32 devices in a mesh: grp: 4 (over z), dp: 8 (over y, x, core).
Axes of the slice: x: 2, y: 2, z: 4, core: 2. Of those that a mesh axis runs over, the one named last changes fastest.
Arguments:
- grads: bfloat16 [4, 8, 8, 8192], P('grp', 'dp'), may hold values from -12 to 12
- momentum: float32 [4, 8, 8, 8192], P('grp', 'dp'), may hold values from -152 to 152
- worker_error: float32 [4, 8, 8, 8192], P('grp', 'dp'), may hold values from -6 to 6
- server_error: float32 [4, 8, 8192], P('grp', 'dp'), may hold values from -2 to 2
Outputs:
- synced: float32 [8, 8192], replicated
- worker_error_out: float32 [4, 8, 8, 8192], P('grp', 'dp')
- server_error_out: float32 [4, 8, 8192], P('grp', 'dp')
The draws below stay inside these ranges and needn't reach their ends.
All inputs are finite; a program needn't handle non-finite values.
Results may differ from the reference program's by a relative error of at most 0.012.
Values may be sent and summed in bfloat16 or wider, within the bound.
A program may use at most 64 MiB of HBM per device.

```python
import math
import jax
import jax.numpy as jnp
from jax import lax

D = 8192
GROUPS = 4
WORKERS = 8
BUCKET_ROWS = 8


def draw_momentum(key, part):
    key_noise, key_rows, key_cols = jax.random.split(key, 3)
    row_factor = jnp.exp(jax.random.uniform(key_rows, (BUCKET_ROWS, 1), jnp.float32, math.log(0.3), math.log(3.0)))
    col_factor = jnp.exp(jax.random.uniform(key_cols, (1, D), jnp.float32, math.log(0.3), math.log(3.0)))
    noise = jnp.clip(jax.random.normal(key_noise, (GROUPS, WORKERS, BUCKET_ROWS, D), jnp.float32), -6.0, 6.0)
    return 2.0 * noise * row_factor * col_factor


def steps_of(rng, shape, cuts, low, high):
    def one(position, blocks):
        heights = jax.random.uniform(jax.random.fold_in(jax.random.fold_in(rng, 6), position), (blocks,), jnp.float32, low / len(cuts), high / len(cuts))
        return jnp.repeat(jnp.exp(heights), shape[position] // blocks).reshape((-1,) + (1,) * (len(shape) - position - 1))

    level = one(*cuts[0])
    for cut in cuts[1:]:
        level = level * one(*cut)
    return level


def normal_values(stream_key, dims, spread, reach, cuts=(), kind=jnp.bfloat16):
    entries = spread * jax.random.normal(stream_key, dims, jnp.float32)
    if cuts:
        entries = entries * steps_of(stream_key, dims, cuts, -0.22, 0.18)
    return jnp.clip(entries, -reach, reach).astype(kind)


def setup_inputs(seed: int = 0) -> dict:
    arg_keys = jax.random.split(jax.random.key(seed), 5)
    grads = normal_values(arg_keys[0], (GROUPS, WORKERS, BUCKET_ROWS, D), 2.0, 12.0, ((0, 4), (1, 8)))
    momentum = draw_momentum(jax.random.fold_in(arg_keys[4], 71), 0)
    worker_error = normal_values(arg_keys[2], (GROUPS, WORKERS, BUCKET_ROWS, D), 1.0, 6.0, ((0, 4), (1, 8)), jnp.float32)
    server_error = normal_values(arg_keys[3], (GROUPS, BUCKET_ROWS, D), 0.3, 2.0, ((0, 4), (1, 8)), jnp.float32)
    return {"grads": grads, "momentum": momentum, "worker_error": worker_error, "server_error": server_error}


def compress(values):
    row_scale = (jnp.mean(jnp.abs(values), axis=-1, keepdims=True) + 1e-6).astype(jnp.bfloat16)
    scale_wide = row_scale.astype(jnp.float32)
    coded = jnp.tanh(values / scale_wide).astype(jnp.bfloat16)
    leftover = values - scale_wide * coded.astype(jnp.float32)
    return row_scale, coded, leftover


def one_group(packed):
    grad_part, moment_part, werr_part, serr_part = packed
    blended = 0.9 * moment_part + 0.1 * grad_part.astype(jnp.float32) + werr_part
    row_scale, coded, werr_new = compress(blended)
    summed = jnp.einsum("wrd,wr->rd", coded.astype(jnp.float32), row_scale[..., 0].astype(jnp.float32))
    server_input = summed / WORKERS + serr_part
    server_scale, server_code, serr_new = compress(server_input)
    decoded = server_scale.astype(jnp.float32) * server_code.astype(jnp.float32)
    return werr_new, serr_new, decoded


def reference(grads, momentum, worker_error, server_error):
    werr_all, serr_all, decoded_all = lax.map(one_group, (grads, momentum, worker_error, server_error))
    synced = jnp.sum(decoded_all, axis=0) / GROUPS
    return synced, werr_all, serr_all
```

```python
import functools

import jax
import jax.numpy as jnp
from jax import lax
from jax.experimental import pallas as pl
from jax.experimental.pallas import tpu as pltpu
from jax.sharding import PartitionSpec as P

MESH = pl.DeviceIdType.MESH
LANES = 128


def each(count, body):
    if count <= 8:
        for k in range(1, count):
            body(k)
    else:
        lax.fori_loop(1, count, lambda k, _: (body(k), None)[1], None)


def wait_bytes(ref, sem):
    pltpu.make_async_copy(ref, ref, sem).wait()


def kernel(
    n, groups, rows, width,
    grads, momentum, worker_error, server_error,
    synced, werr_out, serr_out,
    g_in, m_in, e_in, se_in, blend, code, by_row, werr_st, serr_st, sync_st,
    send, got, scale_send, scale_got, zbuf, gathered,
    in_sem, out_sem, code_sem, scale_sem, z_sem, ag_sem,
):
    me, grp = lax.axis_index("dp"), lax.axis_index("grp")
    tiles = width // LANES

    loads = [
        pltpu.make_async_copy(src, dst, in_sem.at[i])
        for i, (src, dst) in enumerate(
            ((momentum, m_in), (worker_error, e_in), (grads, g_in), (server_error, se_in))
        )
    ]
    for load in loads:
        load.start()

    barrier = pltpu.get_barrier_semaphore()

    def greet_dp(k):
        pl.semaphore_signal(
            barrier, inc=1, device_id=(grp, lax.rem(me + k, n)), device_id_type=MESH
        )

    def greet_grp(k):
        pl.semaphore_signal(
            barrier, inc=1, device_id=(lax.rem(grp + k, groups), me), device_id_type=MESH
        )

    each(n, greet_dp)
    each(groups, greet_grp)

    for load in loads[:3]:
        load.wait()

    total = jnp.zeros((rows, LANES), jnp.float32)
    for t in range(tiles):
        cols = slice(t * LANES, (t + 1) * LANES)
        b = 0.9 * m_in[:, cols] + 0.1 * g_in[:, cols].astype(jnp.float32) + e_in[:, cols]
        blend[:, cols] = b
        total = total + jnp.abs(b)
    mean = jnp.sum(total, axis=1, keepdims=True) / width
    scale = (mean + 1e-6).astype(jnp.bfloat16).astype(jnp.float32)
    inverse = jnp.broadcast_to(1.0 / scale, (rows, LANES))
    scale = jnp.broadcast_to(scale, (rows, LANES))
    for r in range(rows):
        scale_send[r] = scale[r : r + 1]

    pl.semaphore_wait(barrier, n - 1 + groups - 1)

    def send_scale(k):
        to = lax.rem(me + k, n)
        pltpu.make_async_remote_copy(
            src_ref=scale_send.at[to],
            dst_ref=scale_got.at[k - 1],
            send_sem=scale_sem.at[0],
            recv_sem=scale_sem.at[1],
            device_id=(grp, to),
            device_id_type=MESH,
        ).start()

    each(n, send_scale)

    for t in range(tiles):
        cols = slice(t * LANES, (t + 1) * LANES)
        c = jnp.tanh(blend[:, cols] * inverse).astype(jnp.bfloat16).astype(jnp.float32)
        code[:, cols] = c
        by_row[pl.ds(t, rows, stride=tiles), :] = c

    def row_of(r):
        return pl.ds(pl.multiple_of(r * tiles, tiles), tiles)

    def send_code(k):
        to = lax.rem(me + k, n)
        send[k - 1] = by_row[row_of(to), :].astype(jnp.bfloat16)
        pltpu.make_async_remote_copy(
            src_ref=send.at[k - 1],
            dst_ref=got.at[k - 1],
            send_sem=code_sem.at[0],
            recv_sem=code_sem.at[1],
            device_id=(grp, to),
            device_id_type=MESH,
        ).start()

    each(n, send_code)

    for t in range(tiles):
        cols = slice(t * LANES, (t + 1) * LANES)
        werr_st[:, cols] = blend[:, cols] - scale * code[:, cols]
    werr_store = pltpu.make_async_copy(werr_st, werr_out, out_sem.at[0])
    werr_store.start()
    loads[3].wait()

    summed = by_row[row_of(me), :] * scale_send[me]
    wait_bytes(scale_got, scale_sem.at[1])
    wait_bytes(got, code_sem.at[1])
    for k in range(n - 1):
        summed = summed + got[k].astype(jnp.float32) * scale_got[k]
    entry = summed / n + se_in[...]
    mean = jnp.sum(jnp.sum(jnp.abs(entry), axis=0, keepdims=True), axis=1, keepdims=True) / width
    s_scale = (mean + 1e-6).astype(jnp.bfloat16).astype(jnp.float32)
    s_code = jnp.tanh(entry * (1.0 / s_scale)).astype(jnp.bfloat16).astype(jnp.float32)
    decoded = s_scale * s_code
    zbuf[grp] = decoded.astype(jnp.bfloat16)

    def send_z(k):
        pltpu.make_async_remote_copy(
            src_ref=zbuf.at[grp],
            dst_ref=zbuf.at[grp],
            send_sem=z_sem.at[0],
            recv_sem=z_sem.at[1],
            device_id=(lax.rem(grp + k, groups), me),
            device_id_type=MESH,
        ).start()

    each(groups, send_z)
    serr_st[...] = entry - decoded
    serr_store = pltpu.make_async_copy(serr_st, serr_out, out_sem.at[1])
    serr_store.start()

    if groups > 1:
        wait_bytes(zbuf.at[pl.ds(0, groups - 1)], z_sem.at[1])
    mixed = zbuf[0].astype(jnp.float32)
    for g in range(1, groups):
        mixed = mixed + zbuf[g].astype(jnp.float32)
    gathered[me] = (mixed / groups).astype(jnp.bfloat16)

    def send_ag(k):
        pltpu.make_async_remote_copy(
            src_ref=gathered.at[me],
            dst_ref=gathered.at[me],
            send_sem=ag_sem.at[0],
            recv_sem=ag_sem.at[1],
            device_id=(grp, lax.rem(me + k, n)),
            device_id_type=MESH,
        ).start()

    each(n, send_ag)
    wait_bytes(gathered.at[pl.ds(0, n - 1)], ag_sem.at[1])
    for r in range(n):
        by_row[r * tiles : (r + 1) * tiles, :] = gathered[r].astype(jnp.float32)
    for t in range(tiles):
        sync_st[:, t * LANES : (t + 1) * LANES] = by_row[pl.ds(t, rows, stride=tiles), :]
    sync_store = pltpu.make_async_copy(sync_st, synced, out_sem.at[2])
    sync_store.start()

    wait_bytes(scale_got, scale_sem.at[0])
    wait_bytes(got, code_sem.at[0])
    if groups > 1:
        wait_bytes(zbuf.at[pl.ds(0, groups - 1)], z_sem.at[0])
    wait_bytes(gathered.at[pl.ds(0, n - 1)], ag_sem.at[0])
    werr_store.wait()
    serr_store.wait()
    sync_store.wait()


def solution(mesh):
    n, groups = mesh.shape["dp"], mesh.shape["grp"]

    def per_device(grads, momentum, worker_error, server_error):
        rows, width = grads.shape[2:]
        assert rows == n
        tiles = width // LANES
        f32, bf16 = jnp.float32, jnp.bfloat16
        whole = (rows, width)
        block = (tiles, LANES)
        anywhere = pl.BlockSpec(memory_space=pl.ANY)
        synced, werr, serr = pl.pallas_call(
            functools.partial(kernel, n, groups, rows, width),
            out_shape=(
                jax.ShapeDtypeStruct(whole, f32),
                jax.ShapeDtypeStruct(whole, f32),
                jax.ShapeDtypeStruct(block, f32),
            ),
            in_specs=[anywhere] * 4,
            out_specs=(anywhere,) * 3,
            scratch_shapes=[
                pltpu.VMEM(whole, bf16),
                pltpu.VMEM(whole, f32),
                pltpu.VMEM(whole, f32),
                pltpu.VMEM(block, f32),
                pltpu.VMEM(whole, f32),
                pltpu.VMEM(whole, f32),
                pltpu.VMEM((rows * tiles, LANES), f32),
                pltpu.VMEM(whole, f32),
                pltpu.VMEM(block, f32),
                pltpu.VMEM(whole, f32),
                pltpu.VMEM((n - 1,) + block, bf16),
                pltpu.VMEM((n - 1,) + block, bf16),
                pltpu.VMEM((n, 1, LANES), f32),
                pltpu.VMEM((n - 1, 1, LANES), f32),
                pltpu.VMEM((groups,) + block, bf16),
                pltpu.VMEM((n,) + block, bf16),
                pltpu.SemaphoreType.DMA((4,)),
                pltpu.SemaphoreType.DMA((3,)),
                pltpu.SemaphoreType.DMA((2,)),
                pltpu.SemaphoreType.DMA((2,)),
                pltpu.SemaphoreType.DMA((2,)),
                pltpu.SemaphoreType.DMA((2,)),
            ],
            compiler_params=pltpu.CompilerParams(
                collective_id=0, has_side_effects=True, vmem_limit_bytes=48 * 2**20
            ),
            name="sync",
        )(
            grads.reshape(whole),
            momentum.reshape(whole),
            worker_error.reshape(whole),
            server_error.reshape(block),
        )
        return synced, werr.reshape(momentum.shape), serr.reshape(server_error.shape)

    placed = (
        P("grp", "dp", None, None),
        P("grp", "dp", None, None),
        P("grp", "dp", None, None),
        P("grp", "dp", None),
    )
    return jax.shard_map(
        per_device,
        mesh=mesh,
        in_specs=placed,
        out_specs=(P(), P("grp", "dp", None, None), P("grp", "dp", None)),
        check_vma=False,
    )
```

```python
import functools

import jax
import jax.numpy as jnp
from jax import lax
from jax.experimental import pallas as pl
from jax.experimental.pallas import tpu as pltpu
from jax.sharding import PartitionSpec as P

MESH = pl.DeviceIdType.MESH
LANES = 128


def each(count, body):
    if count <= 8:
        for k in range(1, count):
            body(k)
    else:
        lax.fori_loop(1, count, lambda k, _: (body(k), None)[1], None)


def wait_bytes(ref, sem):
    pltpu.make_async_copy(ref, ref, sem).wait()


def kernel(
    n, groups, rows, width,
    grads, momentum, worker_error, server_error,
    synced, werr_out, serr_out,
    g_in, m_in, e_in, se_in, blend, code, by_row,
    send, got, scale_send, scale_got, zbuf, gathered,
    in_sem, code_sem, scale_sem, z_sem, ag_sem,
):
    me, grp = lax.axis_index("dp"), lax.axis_index("grp")
    tiles = width // LANES

    loads = [
        pltpu.make_async_copy(src, dst, in_sem.at[i])
        for i, (src, dst) in enumerate(
            ((momentum, m_in), (worker_error, e_in), (grads, g_in), (server_error, se_in))
        )
    ]
    for load in loads:
        load.start()

    barrier = pltpu.get_barrier_semaphore()

    def greet_dp(k):
        pl.semaphore_signal(
            barrier, inc=1, device_id=(grp, lax.rem(me + k, n)), device_id_type=MESH
        )

    def greet_grp(k):
        pl.semaphore_signal(
            barrier, inc=1, device_id=(lax.rem(grp + k, groups), me), device_id_type=MESH
        )

    each(n, greet_dp)
    each(groups, greet_grp)

    for load in loads[:3]:
        load.wait()

    total = jnp.zeros((rows, LANES), jnp.float32)
    for t in range(tiles):
        cols = slice(t * LANES, (t + 1) * LANES)
        b = 0.9 * m_in[:, cols] + 0.1 * g_in[:, cols].astype(jnp.float32) + e_in[:, cols]
        blend[:, cols] = b
        total = total + jnp.abs(b)
    mean = jnp.sum(total, axis=1, keepdims=True) / width
    scale = (mean + 1e-6).astype(jnp.bfloat16).astype(jnp.float32)
    inverse = jnp.broadcast_to(1.0 / scale, (rows, LANES))
    scale = jnp.broadcast_to(scale, (rows, LANES))
    for r in range(rows):
        scale_send[r] = scale[r : r + 1]

    pl.semaphore_wait(barrier, n - 1 + groups - 1)

    def send_scale(k):
        to = lax.rem(me + k, n)
        pltpu.make_async_remote_copy(
            src_ref=scale_send.at[to],
            dst_ref=scale_got.at[k - 1],
            send_sem=scale_sem.at[0],
            recv_sem=scale_sem.at[1],
            device_id=(grp, to),
            device_id_type=MESH,
        ).start()

    each(n, send_scale)

    for t in range(tiles):
        cols = slice(t * LANES, (t + 1) * LANES)
        c = jnp.tanh(blend[:, cols] * inverse).astype(jnp.bfloat16).astype(jnp.float32)
        code[:, cols] = c
        by_row[pl.ds(t, rows, stride=tiles), :] = c

    def row_of(r):
        return pl.ds(pl.multiple_of(r * tiles, tiles), tiles)

    def send_code(k):
        to = lax.rem(me + k, n)
        send[k - 1] = by_row[row_of(to), :].astype(jnp.bfloat16)
        pltpu.make_async_remote_copy(
            src_ref=send.at[k - 1],
            dst_ref=got.at[k - 1],
            send_sem=code_sem.at[0],
            recv_sem=code_sem.at[1],
            device_id=(grp, to),
            device_id_type=MESH,
        ).start()

    each(n, send_code)

    for t in range(tiles):
        cols = slice(t * LANES, (t + 1) * LANES)
        werr_out[:, cols] = blend[:, cols] - scale * code[:, cols]
    loads[3].wait()

    summed = by_row[row_of(me), :] * scale_send[me]
    wait_bytes(scale_got, scale_sem.at[1])
    wait_bytes(got, code_sem.at[1])
    for k in range(n - 1):
        summed = summed + got[k].astype(jnp.float32) * scale_got[k]
    entry = summed / n + se_in[...]
    mean = jnp.sum(jnp.sum(jnp.abs(entry), axis=0, keepdims=True), axis=1, keepdims=True) / width
    s_scale = (mean + 1e-6).astype(jnp.bfloat16).astype(jnp.float32)
    s_code = jnp.tanh(entry * (1.0 / s_scale)).astype(jnp.bfloat16).astype(jnp.float32)
    decoded = s_scale * s_code
    zbuf[grp] = decoded.astype(jnp.bfloat16)

    def send_z(k):
        pltpu.make_async_remote_copy(
            src_ref=zbuf.at[grp],
            dst_ref=zbuf.at[grp],
            send_sem=z_sem.at[0],
            recv_sem=z_sem.at[1],
            device_id=(lax.rem(grp + k, groups), me),
            device_id_type=MESH,
        ).start()

    each(groups, send_z)
    serr_out[...] = entry - decoded

    if groups > 1:
        wait_bytes(zbuf.at[pl.ds(0, groups - 1)], z_sem.at[1])
    mixed = zbuf[0].astype(jnp.float32)
    for g in range(1, groups):
        mixed = mixed + zbuf[g].astype(jnp.float32)
    gathered[me] = (mixed / groups).astype(jnp.bfloat16)

    def send_ag(k):
        pltpu.make_async_remote_copy(
            src_ref=gathered.at[me],
            dst_ref=gathered.at[me],
            send_sem=ag_sem.at[0],
            recv_sem=ag_sem.at[1],
            device_id=(grp, lax.rem(me + k, n)),
            device_id_type=MESH,
        ).start()

    each(n, send_ag)
    wait_bytes(gathered.at[pl.ds(0, n - 1)], ag_sem.at[1])
    for r in range(n):
        by_row[r * tiles : (r + 1) * tiles, :] = gathered[r].astype(jnp.float32)
    for t in range(tiles):
        synced[:, t * LANES : (t + 1) * LANES] = by_row[pl.ds(t, rows, stride=tiles), :]

    wait_bytes(scale_got, scale_sem.at[0])
    wait_bytes(got, code_sem.at[0])
    if groups > 1:
        wait_bytes(zbuf.at[pl.ds(0, groups - 1)], z_sem.at[0])
    wait_bytes(gathered.at[pl.ds(0, n - 1)], ag_sem.at[0])


def store(synced, werr, serr, synced_out, werr_out, serr_out, sem):
    copies = [
        pltpu.make_async_copy(src, dst, sem.at[i])
        for i, (src, dst) in enumerate(((synced, synced_out), (werr, werr_out), (serr, serr_out)))
    ]
    for copy in copies:
        copy.start()
    for copy in copies:
        copy.wait()


def solution(mesh):
    n, groups = mesh.shape["dp"], mesh.shape["grp"]

    def per_device(grads, momentum, worker_error, server_error):
        rows, width = grads.shape[2:]
        assert rows == n
        tiles = width // LANES
        f32, bf16 = jnp.float32, jnp.bfloat16
        whole = (rows, width)
        block = (tiles, LANES)
        in_hbm = pl.BlockSpec(memory_space=pltpu.HBM)
        in_vmem = pl.BlockSpec(memory_space=pltpu.VMEM)
        anywhere = pl.BlockSpec(memory_space=pl.ANY)
        pinned = functools.partial(pltpu.with_memory_space_constraint, memory_space=pltpu.HBM)
        synced, werr, serr = pl.pallas_call(
            functools.partial(kernel, n, groups, rows, width),
            out_shape=(
                jax.ShapeDtypeStruct(whole, f32),
                jax.ShapeDtypeStruct(whole, f32),
                jax.ShapeDtypeStruct(block, f32),
            ),
            in_specs=[anywhere] * 4,
            out_specs=(in_vmem,) * 3,
            scratch_shapes=[
                pltpu.VMEM(whole, bf16),
                pltpu.VMEM(whole, f32),
                pltpu.VMEM(whole, f32),
                pltpu.VMEM(block, f32),
                pltpu.VMEM(whole, f32),
                pltpu.VMEM(whole, f32),
                pltpu.VMEM((rows * tiles, LANES), f32),
                pltpu.VMEM((n - 1,) + block, bf16),
                pltpu.VMEM((n - 1,) + block, bf16),
                pltpu.VMEM((n, 1, LANES), f32),
                pltpu.VMEM((n - 1, 1, LANES), f32),
                pltpu.VMEM((groups,) + block, bf16),
                pltpu.VMEM((n,) + block, bf16),
                pltpu.SemaphoreType.DMA((4,)),
                pltpu.SemaphoreType.DMA((2,)),
                pltpu.SemaphoreType.DMA((2,)),
                pltpu.SemaphoreType.DMA((2,)),
                pltpu.SemaphoreType.DMA((2,)),
            ],
            compiler_params=pltpu.CompilerParams(
                collective_id=0, has_side_effects=True, vmem_limit_bytes=48 * 2**20
            ),
            name="sync",
        )(
            pinned(grads.reshape(whole)),
            pinned(momentum.reshape(whole)),
            pinned(worker_error.reshape(whole)),
            pinned(server_error.reshape(block)),
        )
        synced, werr, serr = pl.pallas_call(
            store,
            out_shape=tuple(jax.ShapeDtypeStruct(x.shape, f32) for x in (synced, werr, serr)),
            in_specs=[anywhere] * 3,
            out_specs=(in_hbm,) * 3,
            scratch_shapes=[pltpu.SemaphoreType.DMA((3,))],
            name="store",
        )(synced, werr, serr)
        return synced, werr.reshape(momentum.shape), serr.reshape(server_error.shape)

    placed = (
        P("grp", "dp", None, None),
        P("grp", "dp", None, None),
        P("grp", "dp", None, None),
        P("grp", "dp", None),
    )
    return jax.shard_map(
        per_device,
        mesh=mesh,
        in_specs=placed,
        out_specs=(P(), P("grp", "dp", None, None), P("grp", "dp", None)),
        check_vma=False,
    )
```

```python
import functools

import jax
import jax.numpy as jnp
from jax import lax
from jax.experimental import pallas as pl
from jax.experimental.pallas import tpu as pltpu
from jax.sharding import PartitionSpec as P

MESH = pl.DeviceIdType.MESH
LANES = 128


def each(count, body):
    if count <= 8:
        for k in range(1, count):
            body(k)
    else:
        lax.fori_loop(1, count, lambda k, _: (body(k), None)[1], None)


def wait_bytes(ref, sem):
    pltpu.make_async_copy(ref, ref, sem).wait()


def kernel(
    n, groups, rows, width,
    grads, momentum, worker_error, server_error,
    synced, werr_out, serr_out,
    g_in, m_in, e_in, se_in, blend, code, by_row,
    send, got, scale_send, scale_got, zbuf, gathered,
    in_sem, code_sem, scale_sem, z_sem, ag_sem,
):
    me, grp = lax.axis_index("dp"), lax.axis_index("grp")
    tiles = width // LANES

    loads = [
        pltpu.make_async_copy(src, dst, in_sem.at[i])
        for i, (src, dst) in enumerate(
            ((momentum, m_in), (worker_error, e_in), (grads, g_in), (server_error, se_in))
        )
    ]
    for load in loads:
        load.start()

    barrier = pltpu.get_barrier_semaphore()

    def greet_dp(k):
        pl.semaphore_signal(
            barrier, inc=1, device_id=(grp, lax.rem(me + k, n)), device_id_type=MESH
        )

    def greet_grp(k):
        pl.semaphore_signal(
            barrier, inc=1, device_id=(lax.rem(grp + k, groups), me), device_id_type=MESH
        )

    each(n, greet_dp)
    each(groups, greet_grp)

    for load in loads[:3]:
        load.wait()

    total = jnp.zeros((rows, LANES), jnp.float32)
    for t in range(tiles):
        cols = slice(t * LANES, (t + 1) * LANES)
        b = 0.9 * m_in[:, cols] + 0.1 * g_in[:, cols].astype(jnp.float32) + e_in[:, cols]
        blend[:, cols] = b
        total = total + jnp.abs(b)
    mean = jnp.sum(total, axis=1, keepdims=True) / width
    scale = (mean + 1e-6).astype(jnp.bfloat16).astype(jnp.float32)
    inverse = jnp.broadcast_to(1.0 / scale, (rows, LANES))
    scale = jnp.broadcast_to(scale, (rows, LANES))
    for r in range(rows):
        scale_send[r] = scale[r : r + 1]

    pl.semaphore_wait(barrier, n - 1 + groups - 1)

    def send_scale(k):
        to = lax.rem(me + k, n)
        pltpu.make_async_remote_copy(
            src_ref=scale_send.at[to],
            dst_ref=scale_got.at[k - 1],
            send_sem=scale_sem.at[0],
            recv_sem=scale_sem.at[1],
            device_id=(grp, to),
            device_id_type=MESH,
        ).start()

    each(n, send_scale)

    for t in range(tiles):
        cols = slice(t * LANES, (t + 1) * LANES)
        c = jnp.tanh(blend[:, cols] * inverse).astype(jnp.bfloat16).astype(jnp.float32)
        code[:, cols] = c
        by_row[pl.ds(t, rows, stride=tiles), :] = c

    def row_of(r):
        return pl.ds(pl.multiple_of(r * tiles, tiles), tiles)

    def send_code(k):
        to = lax.rem(me + k, n)
        send[k - 1] = by_row[row_of(to), :].astype(jnp.bfloat16)
        pltpu.make_async_remote_copy(
            src_ref=send.at[k - 1],
            dst_ref=got.at[k - 1],
            send_sem=code_sem.at[0],
            recv_sem=code_sem.at[1],
            device_id=(grp, to),
            device_id_type=MESH,
        ).start()

    each(n, send_code)

    for t in range(tiles):
        cols = slice(t * LANES, (t + 1) * LANES)
        werr_out[:, cols] = blend[:, cols] - scale * code[:, cols]
    loads[3].wait()

    summed = by_row[row_of(me), :] * scale_send[me]
    wait_bytes(scale_got, scale_sem.at[1])
    wait_bytes(got, code_sem.at[1])
    for k in range(n - 1):
        summed = summed + got[k].astype(jnp.float32) * scale_got[k]
    entry = summed / n + se_in[...]
    mean = jnp.sum(jnp.sum(jnp.abs(entry), axis=0, keepdims=True), axis=1, keepdims=True) / width
    s_scale = (mean + 1e-6).astype(jnp.bfloat16).astype(jnp.float32)
    s_code = jnp.tanh(entry * (1.0 / s_scale)).astype(jnp.bfloat16).astype(jnp.float32)
    decoded = s_scale * s_code
    zbuf[grp] = decoded.astype(jnp.bfloat16)

    def send_z(k):
        pltpu.make_async_remote_copy(
            src_ref=zbuf.at[grp],
            dst_ref=zbuf.at[grp],
            send_sem=z_sem.at[0],
            recv_sem=z_sem.at[1],
            device_id=(lax.rem(grp + k, groups), me),
            device_id_type=MESH,
        ).start()

    each(groups, send_z)
    serr_out[...] = entry - decoded

    if groups > 1:
        wait_bytes(zbuf.at[pl.ds(0, groups - 1)], z_sem.at[1])
    mixed = zbuf[0].astype(jnp.float32)
    for g in range(1, groups):
        mixed = mixed + zbuf[g].astype(jnp.float32)
    gathered[me] = (mixed / groups).astype(jnp.bfloat16)

    def send_ag(k):
        pltpu.make_async_remote_copy(
            src_ref=gathered.at[me],
            dst_ref=gathered.at[me],
            send_sem=ag_sem.at[0],
            recv_sem=ag_sem.at[1],
            device_id=(grp, lax.rem(me + k, n)),
            device_id_type=MESH,
        ).start()

    each(n, send_ag)
    wait_bytes(gathered.at[pl.ds(0, n - 1)], ag_sem.at[1])
    for r in range(n):
        by_row[r * tiles : (r + 1) * tiles, :] = gathered[r].astype(jnp.float32)
    for t in range(tiles):
        synced[:, t * LANES : (t + 1) * LANES] = by_row[pl.ds(t, rows, stride=tiles), :]

    wait_bytes(scale_got, scale_sem.at[0])
    wait_bytes(got, code_sem.at[0])
    if groups > 1:
        wait_bytes(zbuf.at[pl.ds(0, groups - 1)], z_sem.at[0])
    wait_bytes(gathered.at[pl.ds(0, n - 1)], ag_sem.at[0])


def store(synced, werr, serr, synced_out, werr_out, serr_out, sem):
    copies = [
        pltpu.make_async_copy(src, dst, sem.at[i])
        for i, (src, dst) in enumerate(((synced, synced_out), (werr, werr_out), (serr, serr_out)))
    ]
    for copy in copies:
        copy.start()
    for copy in copies:
        copy.wait()


def solution(mesh):
    n, groups = mesh.shape["dp"], mesh.shape["grp"]

    def per_device(grads, momentum, worker_error, server_error):
        rows, width = grads.shape[2:]
        assert rows == n
        tiles = width // LANES
        f32, bf16 = jnp.float32, jnp.bfloat16
        whole = (rows, width)
        block = (tiles, LANES)
        in_hbm = pl.BlockSpec(memory_space=pltpu.HBM)
        in_vmem = pl.BlockSpec(memory_space=pltpu.VMEM)
        anywhere = pl.BlockSpec(memory_space=pl.ANY)
        pinned = functools.partial(pltpu.with_memory_space_constraint, memory_space=pltpu.HBM)
        synced, werr, serr = pl.pallas_call(
            functools.partial(kernel, n, groups, rows, width),
            out_shape=(
                jax.ShapeDtypeStruct(whole, f32),
                jax.ShapeDtypeStruct(whole, f32),
                jax.ShapeDtypeStruct(block, f32),
            ),
            in_specs=[anywhere] * 4,
            out_specs=(in_vmem,) * 3,
            scratch_shapes=[
                pltpu.VMEM(whole, bf16),
                pltpu.VMEM(whole, f32),
                pltpu.VMEM(whole, f32),
                pltpu.VMEM(block, f32),
                pltpu.VMEM(whole, f32),
                pltpu.VMEM(whole, f32),
                pltpu.VMEM((rows * tiles, LANES), f32),
                pltpu.VMEM((n - 1,) + block, bf16),
                pltpu.VMEM((n - 1,) + block, bf16),
                pltpu.VMEM((n, 1, LANES), f32),
                pltpu.VMEM((n - 1, 1, LANES), f32),
                pltpu.VMEM((groups,) + block, bf16),
                pltpu.VMEM((n,) + block, bf16),
                pltpu.SemaphoreType.DMA((4,)),
                pltpu.SemaphoreType.DMA((2,)),
                pltpu.SemaphoreType.DMA((2,)),
                pltpu.SemaphoreType.DMA((2,)),
                pltpu.SemaphoreType.DMA((2,)),
            ],
            compiler_params=pltpu.CompilerParams(
                collective_id=0, has_side_effects=True, vmem_limit_bytes=48 * 2**20
            ),
            name="sync",
        )(
            pinned(grads.reshape(whole)),
            pinned(momentum.reshape(whole)),
            pinned(worker_error.reshape(whole)),
            pinned(server_error.reshape(block)),
        )
        synced, werr, serr = pl.pallas_call(
            store,
            out_shape=tuple(jax.ShapeDtypeStruct(x.shape, f32) for x in (synced, werr, serr)),
            in_specs=[anywhere] * 3,
            out_specs=(in_hbm,) * 3,
            scratch_shapes=[pltpu.SemaphoreType.DMA((3,))],
            compiler_params=pltpu.CompilerParams(vmem_limit_bytes=2**20),
            name="store",
        )(synced, werr, serr)
        return synced, werr.reshape(momentum.shape), serr.reshape(server_error.shape)

    placed = (
        P("grp", "dp", None, None),
        P("grp", "dp", None, None),
        P("grp", "dp", None, None),
        P("grp", "dp", None),
    )
    return jax.shard_map(
        per_device,
        mesh=mesh,
        in_specs=placed,
        out_specs=(P(), P("grp", "dp", None, None), P("grp", "dp", None)),
        check_vma=False,
    )
```

```python
import functools

import jax
import jax.numpy as jnp
from jax import lax
from jax.experimental import pallas as pl
from jax.experimental.pallas import tpu as pltpu
from jax.sharding import PartitionSpec as P

MESH = pl.DeviceIdType.MESH
LANES = 128


def partners(me, n):
    if n & (n - 1):
        return {k: lax.rem(me + k, n) for k in range(n - 1, 0, -1)}
    flips = [(1 << i, (1 << i) * (1 - 2 * lax.rem(lax.div(me, 1 << i), 2))) for i in range(n.bit_length() - 1)]
    return {k: me + sum(step for bit, step in flips if k & bit) for k in range(n - 1, 0, -1)}


def wait_bytes(ref, sem):
    pltpu.make_async_copy(ref, ref, sem).wait()


def kernel(
    n, groups, rows, width, parts,
    grads, momentum, worker_error, server_error,
    synced, werr_out, serr_out,
    g_in, m_in, e_in, se_in, blend, code, by_row, entry,
    send, got, scale_send, scale_got, zbuf, gathered,
    in_sem, code_sem, scale_sem, z_sem, ag_sem,
):
    me, grp = lax.axis_index("dp"), lax.axis_index("grp")
    tiles = width // LANES
    part = tiles // parts

    loads = [
        pltpu.make_async_copy(src, dst, in_sem.at[i])
        for i, (src, dst) in enumerate(
            ((momentum, m_in), (worker_error, e_in), (grads, g_in), (server_error, se_in))
        )
    ]
    for load in loads:
        load.start()

    mates = partners(me, n)
    others = partners(grp, groups)
    barrier = pltpu.get_barrier_semaphore()
    for to in mates.values():
        pl.semaphore_signal(barrier, inc=1, device_id=(grp, to), device_id_type=MESH)
    for to in others.values():
        pl.semaphore_signal(barrier, inc=1, device_id=(to, me), device_id_type=MESH)

    def push(src, dst, sems, device):
        pltpu.make_async_remote_copy(
            src_ref=src,
            dst_ref=dst,
            send_sem=sems.at[0],
            recv_sem=sems.at[1],
            device_id=device,
            device_id_type=MESH,
        ).start()

    for load in loads[:3]:
        load.wait()

    total = jnp.zeros((rows, LANES), jnp.float32)
    for t in range(tiles):
        cols = slice(t * LANES, (t + 1) * LANES)
        b = 0.9 * m_in[:, cols] + 0.1 * g_in[:, cols].astype(jnp.float32) + e_in[:, cols]
        blend[:, cols] = b
        total = total + jnp.abs(b)
    mean = jnp.sum(total, axis=1, keepdims=True) / width
    scale = (mean + 1e-6).astype(jnp.bfloat16).astype(jnp.float32)
    inverse = jnp.broadcast_to(1.0 / scale, (rows, LANES))
    scale = jnp.broadcast_to(scale, (rows, LANES))
    for r in range(rows):
        scale_send[r] = scale[r : r + 1]

    def block_of(p, r):
        return pl.ds(pl.multiple_of((p * rows + r) * part, part), part)

    for p in range(parts):
        for t in range(part):
            cols = slice((p * part + t) * LANES, (p * part + t + 1) * LANES)
            c = jnp.tanh(blend[:, cols] * inverse).astype(jnp.bfloat16).astype(jnp.float32)
            code[:, cols] = c
            by_row[pl.ds(p * rows * part + t, rows, stride=part), :] = c
        if p == 0:
            pl.semaphore_wait(barrier, n - 1 + groups - 1)
        for k, to in mates.items():
            send[p, k - 1] = by_row[block_of(p, to), :].astype(jnp.bfloat16)
            push(send.at[p, k - 1], got.at[p, k - 1], code_sem.at[p], (grp, to))
        if p == 0:
            for k, to in mates.items():
                push(scale_send.at[to], scale_got.at[k - 1], scale_sem, (grp, to))

    for t in range(tiles):
        cols = slice(t * LANES, (t + 1) * LANES)
        werr_out[:, cols] = blend[:, cols] - scale * code[:, cols]
    loads[3].wait()

    wait_bytes(scale_got, scale_sem.at[1])
    heights = [scale_got[k] for k in range(n - 1)]
    size = jnp.zeros((part, LANES), jnp.float32)
    for p in range(parts):
        here = slice(p * part, (p + 1) * part)
        summed = by_row[block_of(p, me), :] * scale_send[me]
        wait_bytes(got.at[p], code_sem.at[p, 1])
        for k in range(n - 1):
            summed = summed + got[p, k].astype(jnp.float32) * heights[k]
        summed = summed / n + se_in[here, :]
        entry[here, :] = summed
        size = size + jnp.abs(summed)
    mean = jnp.sum(jnp.sum(size, axis=0, keepdims=True), axis=1, keepdims=True) / width
    s_scale = (mean + 1e-6).astype(jnp.bfloat16).astype(jnp.float32)
    s_inverse = 1.0 / s_scale
    for p in range(parts):
        here = slice(p * part, (p + 1) * part)
        s_code = jnp.tanh(entry[here, :] * s_inverse).astype(jnp.bfloat16).astype(jnp.float32)
        decoded = s_scale * s_code
        zbuf[p, grp] = decoded.astype(jnp.bfloat16)
        for to in others.values():
            push(zbuf.at[p, grp], zbuf.at[p, grp], z_sem.at[p], (to, me))
        serr_out[here, :] = entry[here, :] - decoded

    for p in range(parts):
        if groups > 1:
            wait_bytes(zbuf.at[p, pl.ds(0, groups - 1)], z_sem.at[p, 1])
        mixed = zbuf[p, 0].astype(jnp.float32)
        for g in range(1, groups):
            mixed = mixed + zbuf[p, g].astype(jnp.float32)
        gathered[p, me] = (mixed / groups).astype(jnp.bfloat16)
        for to in mates.values():
            push(gathered.at[p, me], gathered.at[p, me], ag_sem.at[p], (grp, to))

    for p in range(parts):
        wait_bytes(gathered.at[p, pl.ds(0, n - 1)], ag_sem.at[p, 1])
        base = p * rows * part
        for r in range(n):
            by_row[base + r * part : base + (r + 1) * part, :] = gathered[p, r].astype(jnp.float32)
        for t in range(part):
            cols = slice((p * part + t) * LANES, (p * part + t + 1) * LANES)
            synced[:, cols] = by_row[pl.ds(base + t, rows, stride=part), :]

    wait_bytes(scale_got, scale_sem.at[0])
    for p in range(parts):
        wait_bytes(got.at[p], code_sem.at[p, 0])
        if groups > 1:
            wait_bytes(zbuf.at[p, pl.ds(0, groups - 1)], z_sem.at[p, 0])
        wait_bytes(gathered.at[p, pl.ds(0, n - 1)], ag_sem.at[p, 0])


def store(synced, werr, serr, synced_out, werr_out, serr_out, sem):
    copies = [
        pltpu.make_async_copy(src, dst, sem.at[i])
        for i, (src, dst) in enumerate(((synced, synced_out), (werr, werr_out), (serr, serr_out)))
    ]
    for copy in copies:
        copy.start()
    for copy in copies:
        copy.wait()


def solution(mesh):
    n, groups = mesh.shape["dp"], mesh.shape["grp"]

    def per_device(grads, momentum, worker_error, server_error):
        rows, width = grads.shape[2:]
        assert rows == n
        tiles = width // LANES
        parts = 2
        part_block = (tiles // parts, LANES)
        f32, bf16 = jnp.float32, jnp.bfloat16
        whole = (rows, width)
        block = (tiles, LANES)
        in_hbm = pl.BlockSpec(memory_space=pltpu.HBM)
        in_vmem = pl.BlockSpec(memory_space=pltpu.VMEM)
        anywhere = pl.BlockSpec(memory_space=pl.ANY)
        pinned = functools.partial(pltpu.with_memory_space_constraint, memory_space=pltpu.HBM)
        synced, werr, serr = pl.pallas_call(
            functools.partial(kernel, n, groups, rows, width, parts),
            out_shape=(
                jax.ShapeDtypeStruct(whole, f32),
                jax.ShapeDtypeStruct(whole, f32),
                jax.ShapeDtypeStruct(block, f32),
            ),
            in_specs=[anywhere] * 4,
            out_specs=(in_vmem,) * 3,
            scratch_shapes=[
                pltpu.VMEM(whole, bf16),
                pltpu.VMEM(whole, f32),
                pltpu.VMEM(whole, f32),
                pltpu.VMEM(block, f32),
                pltpu.VMEM(whole, f32),
                pltpu.VMEM(whole, f32),
                pltpu.VMEM((rows * tiles, LANES), f32),
                pltpu.VMEM(block, f32),
                pltpu.VMEM((parts, n - 1) + part_block, bf16),
                pltpu.VMEM((parts, n - 1) + part_block, bf16),
                pltpu.VMEM((n, 1, LANES), f32),
                pltpu.VMEM((n - 1, 1, LANES), f32),
                pltpu.VMEM((parts, groups) + part_block, bf16),
                pltpu.VMEM((parts, n) + part_block, bf16),
                pltpu.SemaphoreType.DMA((4,)),
                pltpu.SemaphoreType.DMA((parts, 2)),
                pltpu.SemaphoreType.DMA((2,)),
                pltpu.SemaphoreType.DMA((parts, 2)),
                pltpu.SemaphoreType.DMA((parts, 2)),
            ],
            compiler_params=pltpu.CompilerParams(
                collective_id=0, has_side_effects=True, vmem_limit_bytes=48 * 2**20
            ),
            name="sync",
        )(
            pinned(grads.reshape(whole)),
            pinned(momentum.reshape(whole)),
            pinned(worker_error.reshape(whole)),
            pinned(server_error.reshape(block)),
        )
        synced, werr, serr = pl.pallas_call(
            store,
            out_shape=tuple(jax.ShapeDtypeStruct(x.shape, f32) for x in (synced, werr, serr)),
            in_specs=[anywhere] * 3,
            out_specs=(in_hbm,) * 3,
            scratch_shapes=[pltpu.SemaphoreType.DMA((3,))],
            compiler_params=pltpu.CompilerParams(vmem_limit_bytes=2**20),
            name="store",
        )(synced, werr, serr)
        return synced, werr.reshape(momentum.shape), serr.reshape(server_error.shape)

    placed = (
        P("grp", "dp", None, None),
        P("grp", "dp", None, None),
        P("grp", "dp", None, None),
        P("grp", "dp", None),
    )
    return jax.shard_map(
        per_device,
        mesh=mesh,
        in_specs=placed,
        out_specs=(P(), P("grp", "dp", None, None), P("grp", "dp", None)),
        check_vma=False,
    )
```

```python
import functools
import math

import jax
import jax.numpy as jnp
from jax import lax
from jax.experimental import pallas as pl
from jax.experimental.pallas import tpu as pltpu
from jax.sharding import PartitionSpec as P

MESH = pl.DeviceIdType.MESH
LANES = 128


def partners(me, n):
    if n & (n - 1):
        return {k: lax.rem(me + k, n) for k in range(n - 1, 0, -1)}
    flips = [(1 << i, (1 << i) * (1 - 2 * lax.rem(lax.div(me, 1 << i), 2))) for i in range(n.bit_length() - 1)]
    return {k: me + sum(step for bit, step in flips if k & bit) for k in range(n - 1, 0, -1)}


def over_tiles(start, count, body, carry=0):
    batch = math.gcd(count, 8)

    def step(i, held):
        for j in range(batch):
            t = start + i * batch + j
            held = body(t, pl.ds(pl.multiple_of(t * LANES, LANES), LANES), held)
        return held

    return lax.fori_loop(0, count // batch, step, carry)


def wait_bytes(ref, sem):
    pltpu.make_async_copy(ref, ref, sem).wait()


def kernel(
    n, groups, rows, width, parts,
    grads, momentum, worker_error, server_error,
    synced, werr_out, serr_out,
    g_in, m_in, e_in, se_in, blend, code, by_row, entry,
    send, got, scale_send, scale_got, zbuf, gathered,
    in_sem, code_sem, scale_sem, z_sem, ag_sem,
):
    me, grp = lax.axis_index("dp"), lax.axis_index("grp")
    tiles = width // LANES
    part = tiles // parts

    loads = [
        pltpu.make_async_copy(src, dst, in_sem.at[i])
        for i, (src, dst) in enumerate(
            ((momentum, m_in), (worker_error, e_in), (grads, g_in), (server_error, se_in))
        )
    ]
    for load in loads:
        load.start()

    mates = partners(me, n)
    others = partners(grp, groups)
    barrier = pltpu.get_barrier_semaphore()
    for to in mates.values():
        pl.semaphore_signal(barrier, inc=1, device_id=(grp, to), device_id_type=MESH)
    for to in others.values():
        pl.semaphore_signal(barrier, inc=1, device_id=(to, me), device_id_type=MESH)

    def push(src, dst, sems, device):
        pltpu.make_async_remote_copy(
            src_ref=src,
            dst_ref=dst,
            send_sem=sems.at[0],
            recv_sem=sems.at[1],
            device_id=device,
            device_id_type=MESH,
        ).start()

    for load in loads[:3]:
        load.wait()

    def blend_tile(t, cols, total):
        b = 0.9 * m_in[:, cols] + 0.1 * g_in[:, cols].astype(jnp.float32) + e_in[:, cols]
        blend[:, cols] = b
        return total + jnp.abs(b)

    total = over_tiles(0, tiles, blend_tile, jnp.zeros((rows, LANES), jnp.float32))
    mean = jnp.sum(total, axis=1, keepdims=True) / width
    scale = (mean + 1e-6).astype(jnp.bfloat16).astype(jnp.float32)
    inverse = jnp.broadcast_to(1.0 / scale, (rows, LANES))
    scale = jnp.broadcast_to(scale, (rows, LANES))
    for r in range(rows):
        scale_send[r] = scale[r : r + 1]

    def block_of(p, r):
        return pl.ds(pl.multiple_of((p * rows + r) * part, part), part)

    for p in range(parts):

        def code_tile(t, cols, held):
            c = jnp.tanh(blend[:, cols] * inverse).astype(jnp.bfloat16).astype(jnp.float32)
            code[:, cols] = c
            by_row[pl.ds(p * (rows - 1) * part + t, rows, stride=part), :] = c
            return held

        over_tiles(p * part, part, code_tile)
        if p == 0:
            pl.semaphore_wait(barrier, n - 1 + groups - 1)
        for k, to in mates.items():
            send[p, k - 1] = by_row[block_of(p, to), :].astype(jnp.bfloat16)
            push(send.at[p, k - 1], got.at[p, k - 1], code_sem.at[p], (grp, to))
        if p == 0:
            for k, to in mates.items():
                push(scale_send.at[to], scale_got.at[k - 1], scale_sem, (grp, to))

    def error_tile(t, cols, held):
        werr_out[:, cols] = blend[:, cols] - scale * code[:, cols]
        return held

    over_tiles(0, tiles, error_tile)
    loads[3].wait()

    wait_bytes(scale_got, scale_sem.at[1])
    heights = [scale_got[k] for k in range(n - 1)]
    size = jnp.zeros((part, LANES), jnp.float32)
    for p in range(parts):
        here = slice(p * part, (p + 1) * part)
        summed = by_row[block_of(p, me), :] * scale_send[me]
        wait_bytes(got.at[p], code_sem.at[p, 1])
        for k in range(n - 1):
            summed = summed + got[p, k].astype(jnp.float32) * heights[k]
        summed = summed / n + se_in[here, :]
        entry[here, :] = summed
        size = size + jnp.abs(summed)
    mean = jnp.sum(jnp.sum(size, axis=0, keepdims=True), axis=1, keepdims=True) / width
    s_scale = (mean + 1e-6).astype(jnp.bfloat16).astype(jnp.float32)
    s_inverse = 1.0 / s_scale
    for p in range(parts):
        here = slice(p * part, (p + 1) * part)
        s_code = jnp.tanh(entry[here, :] * s_inverse).astype(jnp.bfloat16).astype(jnp.float32)
        decoded = s_scale * s_code
        zbuf[p, grp] = decoded.astype(jnp.bfloat16)
        for to in others.values():
            push(zbuf.at[p, grp], zbuf.at[p, grp], z_sem.at[p], (to, me))
        serr_out[here, :] = entry[here, :] - decoded

    for p in range(parts):
        if groups > 1:
            wait_bytes(zbuf.at[p, pl.ds(0, groups - 1)], z_sem.at[p, 1])
        mixed = zbuf[p, 0].astype(jnp.float32)
        for g in range(1, groups):
            mixed = mixed + zbuf[p, g].astype(jnp.float32)
        gathered[p, me] = (mixed / groups).astype(jnp.bfloat16)
        for to in mates.values():
            push(gathered.at[p, me], gathered.at[p, me], ag_sem.at[p], (grp, to))

    for p in range(parts):
        wait_bytes(gathered.at[p, pl.ds(0, n - 1)], ag_sem.at[p, 1])
        base = p * rows * part
        for r in range(n):
            by_row[base + r * part : base + (r + 1) * part, :] = gathered[p, r].astype(jnp.float32)

        def synced_tile(t, cols, held):
            synced[:, cols] = by_row[pl.ds(base - p * part + t, rows, stride=part), :]
            return held

        over_tiles(p * part, part, synced_tile)

    wait_bytes(scale_got, scale_sem.at[0])
    for p in range(parts):
        wait_bytes(got.at[p], code_sem.at[p, 0])
        if groups > 1:
            wait_bytes(zbuf.at[p, pl.ds(0, groups - 1)], z_sem.at[p, 0])
        wait_bytes(gathered.at[p, pl.ds(0, n - 1)], ag_sem.at[p, 0])


def store(synced, werr, serr, synced_out, werr_out, serr_out, sem):
    copies = [
        pltpu.make_async_copy(src, dst, sem.at[i])
        for i, (src, dst) in enumerate(((synced, synced_out), (werr, werr_out), (serr, serr_out)))
    ]
    for copy in copies:
        copy.start()
    for copy in copies:
        copy.wait()


def solution(mesh):
    n, groups = mesh.shape["dp"], mesh.shape["grp"]

    def per_device(grads, momentum, worker_error, server_error):
        rows, width = grads.shape[2:]
        assert rows == n
        tiles = width // LANES
        parts = 2
        part_block = (tiles // parts, LANES)
        f32, bf16 = jnp.float32, jnp.bfloat16
        whole = (rows, width)
        block = (tiles, LANES)
        in_hbm = pl.BlockSpec(memory_space=pltpu.HBM)
        in_vmem = pl.BlockSpec(memory_space=pltpu.VMEM)
        anywhere = pl.BlockSpec(memory_space=pl.ANY)
        pinned = functools.partial(pltpu.with_memory_space_constraint, memory_space=pltpu.HBM)
        synced, werr, serr = pl.pallas_call(
            functools.partial(kernel, n, groups, rows, width, parts),
            out_shape=(
                jax.ShapeDtypeStruct(whole, f32),
                jax.ShapeDtypeStruct(whole, f32),
                jax.ShapeDtypeStruct(block, f32),
            ),
            in_specs=[anywhere] * 4,
            out_specs=(in_vmem,) * 3,
            scratch_shapes=[
                pltpu.VMEM(whole, bf16),
                pltpu.VMEM(whole, f32),
                pltpu.VMEM(whole, f32),
                pltpu.VMEM(block, f32),
                pltpu.VMEM(whole, f32),
                pltpu.VMEM(whole, f32),
                pltpu.VMEM((rows * tiles, LANES), f32),
                pltpu.VMEM(block, f32),
                pltpu.VMEM((parts, n - 1) + part_block, bf16),
                pltpu.VMEM((parts, n - 1) + part_block, bf16),
                pltpu.VMEM((n, 1, LANES), f32),
                pltpu.VMEM((n - 1, 1, LANES), f32),
                pltpu.VMEM((parts, groups) + part_block, bf16),
                pltpu.VMEM((parts, n) + part_block, bf16),
                pltpu.SemaphoreType.DMA((4,)),
                pltpu.SemaphoreType.DMA((parts, 2)),
                pltpu.SemaphoreType.DMA((2,)),
                pltpu.SemaphoreType.DMA((parts, 2)),
                pltpu.SemaphoreType.DMA((parts, 2)),
            ],
            compiler_params=pltpu.CompilerParams(
                collective_id=0, has_side_effects=True, vmem_limit_bytes=48 * 2**20
            ),
            name="sync",
        )(
            pinned(grads.reshape(whole)),
            pinned(momentum.reshape(whole)),
            pinned(worker_error.reshape(whole)),
            pinned(server_error.reshape(block)),
        )
        synced, werr, serr = pl.pallas_call(
            store,
            out_shape=tuple(jax.ShapeDtypeStruct(x.shape, f32) for x in (synced, werr, serr)),
            in_specs=[anywhere] * 3,
            out_specs=(in_hbm,) * 3,
            scratch_shapes=[pltpu.SemaphoreType.DMA((3,))],
            compiler_params=pltpu.CompilerParams(vmem_limit_bytes=2**20),
            name="store",
        )(synced, werr, serr)
        return synced, werr.reshape(momentum.shape), serr.reshape(server_error.shape)

    placed = (
        P("grp", "dp", None, None),
        P("grp", "dp", None, None),
        P("grp", "dp", None, None),
        P("grp", "dp", None),
    )
    return jax.shard_map(
        per_device,
        mesh=mesh,
        in_specs=placed,
        out_specs=(P(), P("grp", "dp", None, None), P("grp", "dp", None)),
        check_vma=False,
    )
```

```python
import functools
import math

import jax
import jax.numpy as jnp
from jax import lax
from jax.experimental import pallas as pl
from jax.experimental.pallas import tpu as pltpu
from jax.sharding import PartitionSpec as P

MESH = pl.DeviceIdType.MESH
LANES = 128


def partners(me, n):
    if n & (n - 1):
        return {k: lax.rem(me + k, n) for k in range(n - 1, 0, -1)}
    flips = [(1 << i, (1 << i) * (1 - 2 * lax.rem(lax.div(me, 1 << i), 2))) for i in range(n.bit_length() - 1)]
    far = list(range(n - 1, 0, -1))
    half = n // 4
    near = far[: 2 * half]
    order = [k for pair in zip(near[:half], near[half:]) for k in pair] + far[2 * half :]
    return {k: me + sum(step for bit, step in flips if k & bit) for k in order}


def over_tiles(start, count, body, carry=0):
    batch = math.gcd(count, 8)

    def step(i, held):
        for j in range(batch):
            t = start + i * batch + j
            held = body(t, pl.ds(pl.multiple_of(t * LANES, LANES), LANES), held)
        return held

    return lax.fori_loop(0, count // batch, step, carry)


def wait_bytes(ref, sem):
    pltpu.make_async_copy(ref, ref, sem).wait()


def kernel(
    n, groups, rows, width, parts, z_parts,
    grads, momentum, worker_error, server_error,
    synced, werr_out, serr_out,
    g_in, m_in, e_in, se_in, blend, code, by_row, entry,
    send, got, scale_send, scale_got, zbuf, gathered,
    in_sem, code_sem, scale_sem, z_sem, ag_sem,
):
    me, grp = lax.axis_index("dp"), lax.axis_index("grp")
    tiles = width // LANES
    part, z_part = tiles // parts, tiles // z_parts

    loads = [
        pltpu.make_async_copy(src, dst, in_sem.at[i])
        for i, (src, dst) in enumerate(
            ((momentum, m_in), (worker_error, e_in), (grads, g_in), (server_error, se_in))
        )
    ]
    for load in loads:
        load.start()

    mates = partners(me, n)
    others = partners(grp, groups)
    barrier = pltpu.get_barrier_semaphore()
    for to in mates.values():
        pl.semaphore_signal(barrier, inc=1, device_id=(grp, to), device_id_type=MESH)
    for to in others.values():
        pl.semaphore_signal(barrier, inc=1, device_id=(to, me), device_id_type=MESH)

    def push(src, dst, sems, device):
        pltpu.make_async_remote_copy(
            src_ref=src,
            dst_ref=dst,
            send_sem=sems.at[0],
            recv_sem=sems.at[1],
            device_id=device,
            device_id_type=MESH,
        ).start()

    for load in loads[:3]:
        load.wait()

    def blend_tile(t, cols, total):
        b = 0.9 * m_in[:, cols] + 0.1 * g_in[:, cols].astype(jnp.float32) + e_in[:, cols]
        blend[:, cols] = b
        return total + jnp.abs(b)

    total = over_tiles(0, tiles, blend_tile, jnp.zeros((rows, LANES), jnp.float32))
    mean = jnp.sum(total, axis=1, keepdims=True) / width
    scale = (mean + 1e-6).astype(jnp.bfloat16).astype(jnp.float32)
    inverse = jnp.broadcast_to(1.0 / scale, (rows, LANES))
    scale = jnp.broadcast_to(scale, (rows, LANES))
    for r in range(rows):
        scale_send[r] = scale[r : r + 1]

    def block_of(p, r):
        return pl.ds(pl.multiple_of((p * rows + r) * part, part), part)

    for p in range(parts):

        def code_tile(t, cols, held):
            c = jnp.tanh(blend[:, cols] * inverse).astype(jnp.bfloat16).astype(jnp.float32)
            code[:, cols] = c
            by_row[pl.ds(p * (rows - 1) * part + t, rows, stride=part), :] = c
            return held

        over_tiles(p * part, part, code_tile)
        if p == 0:
            pl.semaphore_wait(barrier, n - 1 + groups - 1)
        for k, to in mates.items():
            send[p, k - 1] = by_row[block_of(p, to), :].astype(jnp.bfloat16)
            push(send.at[p, k - 1], got.at[p, k - 1], code_sem.at[p], (grp, to))
        if p == 0:
            for k, to in mates.items():
                push(scale_send.at[to], scale_got.at[k - 1], scale_sem, (grp, to))

    def error_tile(t, cols, held):
        werr_out[:, cols] = blend[:, cols] - scale * code[:, cols]
        return held

    over_tiles(0, tiles, error_tile)
    loads[3].wait()

    wait_bytes(scale_got, scale_sem.at[1])
    heights = [scale_got[k] for k in range(n - 1)]
    size = jnp.zeros((part, LANES), jnp.float32)
    for p in range(parts):
        here = slice(p * part, (p + 1) * part)
        summed = by_row[block_of(p, me), :] * scale_send[me]
        wait_bytes(got.at[p], code_sem.at[p, 1])
        for k in range(n - 1):
            summed = summed + got[p, k].astype(jnp.float32) * heights[k]
        summed = summed / n + se_in[here, :]
        entry[here, :] = summed
        size = size + jnp.abs(summed)
    mean = jnp.sum(jnp.sum(size, axis=0, keepdims=True), axis=1, keepdims=True) / width
    s_scale = (mean + 1e-6).astype(jnp.bfloat16).astype(jnp.float32)
    s_inverse = 1.0 / s_scale
    for p in range(z_parts):
        here = slice(p * z_part, (p + 1) * z_part)
        s_code = jnp.tanh(entry[here, :] * s_inverse).astype(jnp.bfloat16).astype(jnp.float32)
        decoded = s_scale * s_code
        zbuf[p, grp] = decoded.astype(jnp.bfloat16)
        for to in others.values():
            push(zbuf.at[p, grp], zbuf.at[p, grp], z_sem.at[p], (to, me))
        serr_out[here, :] = entry[here, :] - decoded

    for p in range(z_parts):
        if groups > 1:
            wait_bytes(zbuf.at[p, pl.ds(0, groups - 1)], z_sem.at[p, 1])
        mixed = zbuf[p, 0].astype(jnp.float32)
        for g in range(1, groups):
            mixed = mixed + zbuf[p, g].astype(jnp.float32)
        gathered[p, me] = (mixed / groups).astype(jnp.bfloat16)
        for to in mates.values():
            push(gathered.at[p, me], gathered.at[p, me], ag_sem.at[p], (grp, to))

    for p in range(z_parts):
        wait_bytes(gathered.at[p, pl.ds(0, n - 1)], ag_sem.at[p, 1])
        base = p * rows * z_part
        for r in range(n):
            by_row[base + r * z_part : base + (r + 1) * z_part, :] = gathered[p, r].astype(jnp.float32)

        def synced_tile(t, cols, held):
            synced[:, cols] = by_row[pl.ds(base - p * z_part + t, rows, stride=z_part), :]
            return held

        over_tiles(p * z_part, z_part, synced_tile)

    wait_bytes(scale_got, scale_sem.at[0])
    for p in range(parts):
        wait_bytes(got.at[p], code_sem.at[p, 0])
    for p in range(z_parts):
        if groups > 1:
            wait_bytes(zbuf.at[p, pl.ds(0, groups - 1)], z_sem.at[p, 0])
        wait_bytes(gathered.at[p, pl.ds(0, n - 1)], ag_sem.at[p, 0])


def store(synced, werr, serr, synced_out, werr_out, serr_out, sem):
    copies = [
        pltpu.make_async_copy(src, dst, sem.at[i])
        for i, (src, dst) in enumerate(((synced, synced_out), (werr, werr_out), (serr, serr_out)))
    ]
    for copy in copies:
        copy.start()
    for copy in copies:
        copy.wait()


def solution(mesh):
    n, groups = mesh.shape["dp"], mesh.shape["grp"]

    def per_device(grads, momentum, worker_error, server_error):
        rows, width = grads.shape[2:]
        assert rows == n
        tiles = width // LANES
        parts, z_parts = 2, 4
        part_block = (tiles // parts, LANES)
        z_block = (tiles // z_parts, LANES)
        f32, bf16 = jnp.float32, jnp.bfloat16
        whole = (rows, width)
        block = (tiles, LANES)
        in_hbm = pl.BlockSpec(memory_space=pltpu.HBM)
        in_vmem = pl.BlockSpec(memory_space=pltpu.VMEM)
        anywhere = pl.BlockSpec(memory_space=pl.ANY)
        pinned = functools.partial(pltpu.with_memory_space_constraint, memory_space=pltpu.HBM)
        synced, werr, serr = pl.pallas_call(
            functools.partial(kernel, n, groups, rows, width, parts, z_parts),
            out_shape=(
                jax.ShapeDtypeStruct(whole, f32),
                jax.ShapeDtypeStruct(whole, f32),
                jax.ShapeDtypeStruct(block, f32),
            ),
            in_specs=[anywhere] * 4,
            out_specs=(in_vmem,) * 3,
            scratch_shapes=[
                pltpu.VMEM(whole, bf16),
                pltpu.VMEM(whole, f32),
                pltpu.VMEM(whole, f32),
                pltpu.VMEM(block, f32),
                pltpu.VMEM(whole, f32),
                pltpu.VMEM(whole, f32),
                pltpu.VMEM((rows * tiles, LANES), f32),
                pltpu.VMEM(block, f32),
                pltpu.VMEM((parts, n - 1) + part_block, bf16),
                pltpu.VMEM((parts, n - 1) + part_block, bf16),
                pltpu.VMEM((n, 1, LANES), f32),
                pltpu.VMEM((n - 1, 1, LANES), f32),
                pltpu.VMEM((z_parts, groups) + z_block, bf16),
                pltpu.VMEM((z_parts, n) + z_block, bf16),
                pltpu.SemaphoreType.DMA((4,)),
                pltpu.SemaphoreType.DMA((parts, 2)),
                pltpu.SemaphoreType.DMA((2,)),
                pltpu.SemaphoreType.DMA((z_parts, 2)),
                pltpu.SemaphoreType.DMA((z_parts, 2)),
            ],
            compiler_params=pltpu.CompilerParams(
                collective_id=0, has_side_effects=True, vmem_limit_bytes=48 * 2**20
            ),
            name="sync",
        )(
            pinned(grads.reshape(whole)),
            pinned(momentum.reshape(whole)),
            pinned(worker_error.reshape(whole)),
            pinned(server_error.reshape(block)),
        )
        synced, werr, serr = pl.pallas_call(
            store,
            out_shape=tuple(jax.ShapeDtypeStruct(x.shape, f32) for x in (synced, werr, serr)),
            in_specs=[anywhere] * 3,
            out_specs=(in_hbm,) * 3,
            scratch_shapes=[pltpu.SemaphoreType.DMA((3,))],
            compiler_params=pltpu.CompilerParams(vmem_limit_bytes=2**20),
            name="store",
        )(synced, werr, serr)
        return synced, werr.reshape(momentum.shape), serr.reshape(server_error.shape)

    placed = (
        P("grp", "dp", None, None),
        P("grp", "dp", None, None),
        P("grp", "dp", None, None),
        P("grp", "dp", None),
    )
    return jax.shard_map(
        per_device,
        mesh=mesh,
        in_specs=placed,
        out_specs=(P(), P("grp", "dp", None, None), P("grp", "dp", None)),
        check_vma=False,
    )
```

```python
import functools
import math

import jax
import jax.numpy as jnp
from jax import lax
from jax.experimental import pallas as pl
from jax.experimental.pallas import tpu as pltpu
from jax.sharding import PartitionSpec as P

MESH = pl.DeviceIdType.MESH
LANES = 128


def partners(me, n):
    if n & (n - 1):
        return {k: lax.rem(me + k, n) for k in range(n - 1, 0, -1)}
    flips = [(1 << i, (1 << i) * (1 - 2 * lax.rem(lax.div(me, 1 << i), 2))) for i in range(n.bit_length() - 1)]
    far = list(range(n - 1, 0, -1))
    half = n // 4
    near = far[: 2 * half]
    order = [k for pair in zip(near[:half], near[half:]) for k in pair] + far[2 * half :]
    return {k: me + sum(step for bit, step in flips if k & bit) for k in order}


def over_tiles(start, count, body, carry=0):
    batch = math.gcd(count, 8)

    def step(i, held):
        for j in range(batch):
            t = start + i * batch + j
            held = body(t, pl.ds(pl.multiple_of(t * LANES, LANES), LANES), held)
        return held

    return lax.fori_loop(0, count // batch, step, carry)


def wait_bytes(ref, sem):
    pltpu.make_async_copy(ref, ref, sem).wait()


def kernel(
    n, groups, rows, width, parts, z_parts,
    grads, momentum, worker_error, server_error,
    synced, werr_out, serr_out,
    g_in, m_in, e_in, se_in, blend, code, by_row, entry,
    send, got, scale_send, scale_got, zbuf, gathered,
    in_sem, code_sem, scale_sem, z_sem, ag_sem,
):
    me, grp = lax.axis_index("dp"), lax.axis_index("grp")
    tiles = width // LANES
    part, z_part = tiles // parts, tiles // z_parts

    loads = [
        pltpu.make_async_copy(src, dst, in_sem.at[i])
        for i, (src, dst) in enumerate(
            ((momentum, m_in), (worker_error, e_in), (grads, g_in), (server_error, se_in))
        )
    ]
    mates = partners(me, n)
    others = partners(grp, groups)
    barrier = pltpu.get_barrier_semaphore()
    for to in mates.values():
        pl.semaphore_signal(barrier, inc=1, device_id=(grp, to), device_id_type=MESH)
    for to in others.values():
        pl.semaphore_signal(barrier, inc=1, device_id=(to, me), device_id_type=MESH)
    for load in loads:
        load.start()

    def push(src, dst, sems, device):
        pltpu.make_async_remote_copy(
            src_ref=src,
            dst_ref=dst,
            send_sem=sems.at[0],
            recv_sem=sems.at[1],
            device_id=device,
            device_id_type=MESH,
        ).start()

    for load in loads[:3]:
        load.wait()

    def blend_tile(t, cols, total):
        b = 0.9 * m_in[:, cols] + 0.1 * g_in[:, cols].astype(jnp.float32) + e_in[:, cols]
        blend[:, cols] = b
        return total + jnp.abs(b)

    total = over_tiles(0, tiles, blend_tile, jnp.zeros((rows, LANES), jnp.float32))
    mean = jnp.sum(total, axis=1, keepdims=True) / width
    scale = (mean + 1e-6).astype(jnp.bfloat16).astype(jnp.float32)
    inverse = jnp.broadcast_to(1.0 / scale, (rows, LANES))
    scale = jnp.broadcast_to(scale, (rows, LANES))
    for r in range(rows):
        scale_send[r] = scale[r : r + 1]

    def block_of(p, r):
        return pl.ds(pl.multiple_of((p * rows + r) * part, part), part)

    for p in range(parts):

        def code_tile(t, cols, held):
            c = jnp.tanh(blend[:, cols] * inverse).astype(jnp.bfloat16).astype(jnp.float32)
            code[:, cols] = c
            by_row[pl.ds(p * (rows - 1) * part + t, rows, stride=part), :] = c
            return held

        over_tiles(p * part, part, code_tile)
        for k, to in mates.items():
            send[p, k - 1] = by_row[block_of(p, to), :].astype(jnp.bfloat16)

    pl.semaphore_wait(barrier, n - 1 + groups - 1)
    for p in range(parts):
        for k, to in mates.items():
            push(send.at[p, k - 1], got.at[p, k - 1], code_sem.at[p], (grp, to))
    for k, to in mates.items():
        push(scale_send.at[to], scale_got.at[k - 1], scale_sem, (grp, to))

    def error_tile(t, cols, held):
        werr_out[:, cols] = blend[:, cols] - scale * code[:, cols]
        return held

    over_tiles(0, tiles, error_tile)
    loads[3].wait()

    wait_bytes(scale_got, scale_sem.at[1])
    heights = [scale_got[k] for k in range(n - 1)]
    size = jnp.zeros((part, LANES), jnp.float32)
    for p in range(parts):
        here = slice(p * part, (p + 1) * part)
        summed = by_row[block_of(p, me), :] * scale_send[me]
        wait_bytes(got.at[p], code_sem.at[p, 1])
        for k in range(n - 1):
            summed = summed + got[p, k].astype(jnp.float32) * heights[k]
        summed = summed / n + se_in[here, :]
        entry[here, :] = summed
        size = size + jnp.abs(summed)
    mean = jnp.sum(jnp.sum(size, axis=0, keepdims=True), axis=1, keepdims=True) / width
    s_scale = (mean + 1e-6).astype(jnp.bfloat16).astype(jnp.float32)
    s_inverse = 1.0 / s_scale
    for p in range(z_parts):
        here = slice(p * z_part, (p + 1) * z_part)
        s_code = jnp.tanh(entry[here, :] * s_inverse).astype(jnp.bfloat16).astype(jnp.float32)
        decoded = s_scale * s_code
        zbuf[p, grp] = decoded.astype(jnp.bfloat16)
        for to in others.values():
            push(zbuf.at[p, grp], zbuf.at[p, grp], z_sem.at[p], (to, me))
        serr_out[here, :] = entry[here, :] - decoded

    for p in range(z_parts):
        if groups > 1:
            wait_bytes(zbuf.at[p, pl.ds(0, groups - 1)], z_sem.at[p, 1])
        mixed = zbuf[p, 0].astype(jnp.float32)
        for g in range(1, groups):
            mixed = mixed + zbuf[p, g].astype(jnp.float32)
        gathered[p, me] = (mixed / groups).astype(jnp.bfloat16)
        for to in mates.values():
            push(gathered.at[p, me], gathered.at[p, me], ag_sem.at[p], (grp, to))

    for p in range(z_parts):
        wait_bytes(gathered.at[p, pl.ds(0, n - 1)], ag_sem.at[p, 1])
        base = p * rows * z_part
        for r in range(n):
            by_row[base + r * z_part : base + (r + 1) * z_part, :] = gathered[p, r].astype(jnp.float32)

        def synced_tile(t, cols, held):
            synced[:, cols] = by_row[pl.ds(base - p * z_part + t, rows, stride=z_part), :]
            return held

        over_tiles(p * z_part, z_part, synced_tile)

    wait_bytes(scale_got, scale_sem.at[0])
    for p in range(parts):
        wait_bytes(got.at[p], code_sem.at[p, 0])
    for p in range(z_parts):
        if groups > 1:
            wait_bytes(zbuf.at[p, pl.ds(0, groups - 1)], z_sem.at[p, 0])
        wait_bytes(gathered.at[p, pl.ds(0, n - 1)], ag_sem.at[p, 0])


def store(synced, werr, serr, synced_out, werr_out, serr_out, sem):
    copies = [
        pltpu.make_async_copy(src, dst, sem.at[i])
        for i, (src, dst) in enumerate(((synced, synced_out), (werr, werr_out), (serr, serr_out)))
    ]
    for copy in copies:
        copy.start()
    for copy in copies:
        copy.wait()


def solution(mesh):
    n, groups = mesh.shape["dp"], mesh.shape["grp"]

    def per_device(grads, momentum, worker_error, server_error):
        rows, width = grads.shape[2:]
        assert rows == n
        tiles = width // LANES
        parts, z_parts = 1, 2
        part_block = (tiles // parts, LANES)
        z_block = (tiles // z_parts, LANES)
        f32, bf16 = jnp.float32, jnp.bfloat16
        whole = (rows, width)
        block = (tiles, LANES)
        in_hbm = pl.BlockSpec(memory_space=pltpu.HBM)
        in_vmem = pl.BlockSpec(memory_space=pltpu.VMEM)
        anywhere = pl.BlockSpec(memory_space=pl.ANY)
        pinned = functools.partial(pltpu.with_memory_space_constraint, memory_space=pltpu.HBM)
        synced, werr, serr = pl.pallas_call(
            functools.partial(kernel, n, groups, rows, width, parts, z_parts),
            out_shape=(
                jax.ShapeDtypeStruct(whole, f32),
                jax.ShapeDtypeStruct(whole, f32),
                jax.ShapeDtypeStruct(block, f32),
            ),
            in_specs=[anywhere] * 4,
            out_specs=(in_vmem,) * 3,
            scratch_shapes=[
                pltpu.VMEM(whole, bf16),
                pltpu.VMEM(whole, f32),
                pltpu.VMEM(whole, f32),
                pltpu.VMEM(block, f32),
                pltpu.VMEM(whole, f32),
                pltpu.VMEM(whole, f32),
                pltpu.VMEM((rows * tiles, LANES), f32),
                pltpu.VMEM(block, f32),
                pltpu.VMEM((parts, n - 1) + part_block, bf16),
                pltpu.VMEM((parts, n - 1) + part_block, bf16),
                pltpu.VMEM((n, 1, LANES), f32),
                pltpu.VMEM((n - 1, 1, LANES), f32),
                pltpu.VMEM((z_parts, groups) + z_block, bf16),
                pltpu.VMEM((z_parts, n) + z_block, bf16),
                pltpu.SemaphoreType.DMA((4,)),
                pltpu.SemaphoreType.DMA((parts, 2)),
                pltpu.SemaphoreType.DMA((2,)),
                pltpu.SemaphoreType.DMA((z_parts, 2)),
                pltpu.SemaphoreType.DMA((z_parts, 2)),
            ],
            compiler_params=pltpu.CompilerParams(
                collective_id=0, has_side_effects=True, vmem_limit_bytes=48 * 2**20
            ),
            name="sync",
        )(
            pinned(grads.reshape(whole)),
            pinned(momentum.reshape(whole)),
            pinned(worker_error.reshape(whole)),
            pinned(server_error.reshape(block)),
        )
        synced, werr, serr = pl.pallas_call(
            store,
            out_shape=tuple(jax.ShapeDtypeStruct(x.shape, f32) for x in (synced, werr, serr)),
            in_specs=[anywhere] * 3,
            out_specs=(in_hbm,) * 3,
            scratch_shapes=[pltpu.SemaphoreType.DMA((3,))],
            compiler_params=pltpu.CompilerParams(vmem_limit_bytes=2**20),
            name="store",
        )(synced, werr, serr)
        return synced, werr.reshape(momentum.shape), serr.reshape(server_error.shape)

    placed = (
        P("grp", "dp", None, None),
        P("grp", "dp", None, None),
        P("grp", "dp", None, None),
        P("grp", "dp", None),
    )
    return jax.shard_map(
        per_device,
        mesh=mesh,
        in_specs=placed,
        out_specs=(P(), P("grp", "dp", None, None), P("grp", "dp", None)),
        check_vma=False,
    )
```

```python
import functools
import math

import jax
import jax.numpy as jnp
from jax import lax
from jax.experimental import pallas as pl
from jax.experimental.pallas import tpu as pltpu
from jax.sharding import PartitionSpec as P

MESH = pl.DeviceIdType.MESH
LANES = 128


def partners(me, n):
    if n & (n - 1):
        return {k: lax.rem(me + k, n) for k in range(n - 1, 0, -1)}
    flips = [(1 << i, (1 << i) * (1 - 2 * lax.rem(lax.div(me, 1 << i), 2))) for i in range(n.bit_length() - 1)]
    far = list(range(n - 1, 0, -1))
    half = n // 4
    near = far[: 2 * half]
    order = [k for pair in zip(near[:half], near[half:]) for k in pair] + far[2 * half :]
    return {k: me + sum(step for bit, step in flips if k & bit) for k in order}


def over_tiles(start, count, body, carry=0):
    batch = math.gcd(count, 8)

    def step(i, held):
        for j in range(batch):
            t = start + i * batch + j
            held = body(t, pl.ds(pl.multiple_of(t * LANES, LANES), LANES), held)
        return held

    return lax.fori_loop(0, count // batch, step, carry)


def wait_bytes(ref, sem):
    pltpu.make_async_copy(ref, ref, sem).wait()


def kernel(
    n, groups, rows, width, parts, z_parts,
    grads, momentum, worker_error, server_error,
    synced, werr_out, serr_out,
    g_in, m_in, e_in, se_in, blend, decoded_in, by_row, entry,
    send, got, zbuf, gathered,
    in_sem, row_sem, z_sem, ag_sem,
):
    me, grp = lax.axis_index("dp"), lax.axis_index("grp")
    tiles = width // LANES
    part, z_part = tiles // parts, tiles // z_parts

    loads = [
        pltpu.make_async_copy(src, dst, in_sem.at[i])
        for i, (src, dst) in enumerate(
            ((momentum, m_in), (worker_error, e_in), (grads, g_in), (server_error, se_in))
        )
    ]
    mates = partners(me, n)
    others = partners(grp, groups)
    barrier = pltpu.get_barrier_semaphore()
    for to in mates.values():
        pl.semaphore_signal(barrier, inc=1, device_id=(grp, to), device_id_type=MESH)
    for to in others.values():
        pl.semaphore_signal(barrier, inc=1, device_id=(to, me), device_id_type=MESH)
    for load in loads:
        load.start()

    def push(src, dst, sems, device):
        pltpu.make_async_remote_copy(
            src_ref=src,
            dst_ref=dst,
            send_sem=sems.at[0],
            recv_sem=sems.at[1],
            device_id=device,
            device_id_type=MESH,
        ).start()

    for load in loads[:3]:
        load.wait()

    def blend_tile(t, cols, total):
        b = 0.9 * m_in[:, cols] + 0.1 * g_in[:, cols].astype(jnp.float32) + e_in[:, cols]
        blend[:, cols] = b
        return total + jnp.abs(b)

    total = over_tiles(0, tiles, blend_tile, jnp.zeros((rows, LANES), jnp.float32))
    mean = jnp.sum(total, axis=1, keepdims=True) / width
    scale = (mean + 1e-6).astype(jnp.bfloat16).astype(jnp.float32)
    inverse = jnp.broadcast_to(1.0 / scale, (rows, LANES))
    scale = jnp.broadcast_to(scale, (rows, LANES))

    def block_of(p, r):
        return pl.ds(pl.multiple_of((p * rows + r) * part, part), part)

    for p in range(parts):

        def decode_tile(t, cols, held):
            c = jnp.tanh(blend[:, cols] * inverse).astype(jnp.bfloat16).astype(jnp.float32)
            c = scale * c
            decoded_in[:, cols] = c
            by_row[pl.ds(p * (rows - 1) * part + t, rows, stride=part), :] = c
            return held

        over_tiles(p * part, part, decode_tile)
        for k, to in mates.items():
            send[p, k - 1] = by_row[block_of(p, to), :].astype(jnp.bfloat16)

    pl.semaphore_wait(barrier, n - 1 + groups - 1)
    for p in range(parts):
        for k, to in mates.items():
            push(send.at[p, k - 1], got.at[p, k - 1], row_sem.at[p], (grp, to))

    def error_tile(t, cols, held):
        werr_out[:, cols] = blend[:, cols] - decoded_in[:, cols]
        return held

    over_tiles(0, tiles, error_tile)
    loads[3].wait()

    size = jnp.zeros((part, LANES), jnp.float32)
    for p in range(parts):
        here = slice(p * part, (p + 1) * part)
        summed = by_row[block_of(p, me), :]
        wait_bytes(got.at[p], row_sem.at[p, 1])
        for k in range(n - 1):
            summed = summed + got[p, k].astype(jnp.float32)
        summed = summed / n + se_in[here, :]
        entry[here, :] = summed
        size = size + jnp.abs(summed)
    mean = jnp.sum(jnp.sum(size, axis=0, keepdims=True), axis=1, keepdims=True) / width
    s_scale = (mean + 1e-6).astype(jnp.bfloat16).astype(jnp.float32)
    s_inverse = 1.0 / s_scale
    for p in range(z_parts):
        here = slice(p * z_part, (p + 1) * z_part)
        s_code = jnp.tanh(entry[here, :] * s_inverse).astype(jnp.bfloat16).astype(jnp.float32)
        decoded = s_scale * s_code
        zbuf[p, grp] = decoded.astype(jnp.bfloat16)
        for to in others.values():
            push(zbuf.at[p, grp], zbuf.at[p, grp], z_sem.at[p], (to, me))
        serr_out[here, :] = entry[here, :] - decoded

    for p in range(z_parts):
        if groups > 1:
            wait_bytes(zbuf.at[p, pl.ds(0, groups - 1)], z_sem.at[p, 1])
        mixed = zbuf[p, 0].astype(jnp.float32)
        for g in range(1, groups):
            mixed = mixed + zbuf[p, g].astype(jnp.float32)
        gathered[p, me] = (mixed / groups).astype(jnp.bfloat16)
        for to in mates.values():
            push(gathered.at[p, me], gathered.at[p, me], ag_sem.at[p], (grp, to))

    for p in range(z_parts):
        wait_bytes(gathered.at[p, pl.ds(0, n - 1)], ag_sem.at[p, 1])
        base = p * rows * z_part
        for r in range(n):
            by_row[base + r * z_part : base + (r + 1) * z_part, :] = gathered[p, r].astype(jnp.float32)

        def synced_tile(t, cols, held):
            synced[:, cols] = by_row[pl.ds(base - p * z_part + t, rows, stride=z_part), :]
            return held

        over_tiles(p * z_part, z_part, synced_tile)

    for p in range(parts):
        wait_bytes(got.at[p], row_sem.at[p, 0])
    for p in range(z_parts):
        if groups > 1:
            wait_bytes(zbuf.at[p, pl.ds(0, groups - 1)], z_sem.at[p, 0])
        wait_bytes(gathered.at[p, pl.ds(0, n - 1)], ag_sem.at[p, 0])


def store(synced, werr, serr, synced_out, werr_out, serr_out, sem):
    copies = [
        pltpu.make_async_copy(src, dst, sem.at[i])
        for i, (src, dst) in enumerate(((synced, synced_out), (werr, werr_out), (serr, serr_out)))
    ]
    for copy in copies:
        copy.start()
    for copy in copies:
        copy.wait()


def solution(mesh):
    n, groups = mesh.shape["dp"], mesh.shape["grp"]

    def per_device(grads, momentum, worker_error, server_error):
        rows, width = grads.shape[2:]
        assert rows == n
        tiles = width // LANES
        parts, z_parts = 1, 2
        part_block = (tiles // parts, LANES)
        z_block = (tiles // z_parts, LANES)
        f32, bf16 = jnp.float32, jnp.bfloat16
        whole = (rows, width)
        block = (tiles, LANES)
        in_hbm = pl.BlockSpec(memory_space=pltpu.HBM)
        in_vmem = pl.BlockSpec(memory_space=pltpu.VMEM)
        anywhere = pl.BlockSpec(memory_space=pl.ANY)
        pinned = functools.partial(pltpu.with_memory_space_constraint, memory_space=pltpu.HBM)
        synced, werr, serr = pl.pallas_call(
            functools.partial(kernel, n, groups, rows, width, parts, z_parts),
            out_shape=(
                jax.ShapeDtypeStruct(whole, f32),
                jax.ShapeDtypeStruct(whole, f32),
                jax.ShapeDtypeStruct(block, f32),
            ),
            in_specs=[anywhere] * 4,
            out_specs=(in_vmem,) * 3,
            scratch_shapes=[
                pltpu.VMEM(whole, bf16),
                pltpu.VMEM(whole, f32),
                pltpu.VMEM(whole, f32),
                pltpu.VMEM(block, f32),
                pltpu.VMEM(whole, f32),
                pltpu.VMEM(whole, f32),
                pltpu.VMEM((rows * tiles, LANES), f32),
                pltpu.VMEM(block, f32),
                pltpu.VMEM((parts, n - 1) + part_block, bf16),
                pltpu.VMEM((parts, n - 1) + part_block, bf16),
                pltpu.VMEM((z_parts, groups) + z_block, bf16),
                pltpu.VMEM((z_parts, n) + z_block, bf16),
                pltpu.SemaphoreType.DMA((4,)),
                pltpu.SemaphoreType.DMA((parts, 2)),
                pltpu.SemaphoreType.DMA((z_parts, 2)),
                pltpu.SemaphoreType.DMA((z_parts, 2)),
            ],
            compiler_params=pltpu.CompilerParams(
                collective_id=0, has_side_effects=True, vmem_limit_bytes=48 * 2**20
            ),
            name="sync",
        )(
            pinned(grads.reshape(whole)),
            pinned(momentum.reshape(whole)),
            pinned(worker_error.reshape(whole)),
            pinned(server_error.reshape(block)),
        )
        synced, werr, serr = pl.pallas_call(
            store,
            out_shape=tuple(jax.ShapeDtypeStruct(x.shape, f32) for x in (synced, werr, serr)),
            in_specs=[anywhere] * 3,
            out_specs=(in_hbm,) * 3,
            scratch_shapes=[pltpu.SemaphoreType.DMA((3,))],
            compiler_params=pltpu.CompilerParams(vmem_limit_bytes=2**20),
            name="store",
        )(synced, werr, serr)
        return synced, werr.reshape(momentum.shape), serr.reshape(server_error.shape)

    placed = (
        P("grp", "dp", None, None),
        P("grp", "dp", None, None),
        P("grp", "dp", None, None),
        P("grp", "dp", None),
    )
    return jax.shard_map(
        per_device,
        mesh=mesh,
        in_specs=placed,
        out_specs=(P(), P("grp", "dp", None, None), P("grp", "dp", None)),
        check_vma=False,
    )
```

```python
import functools
import math

import jax
import jax.numpy as jnp
from jax import lax
from jax.experimental import pallas as pl
from jax.experimental.pallas import tpu as pltpu
from jax.sharding import PartitionSpec as P

MESH = pl.DeviceIdType.MESH
LANES = 128


def partners(me, n):
    if n & (n - 1):
        return {k: lax.rem(me + k, n) for k in range(n - 1, 0, -1)}
    flips = [(1 << i, (1 << i) * (1 - 2 * lax.rem(lax.div(me, 1 << i), 2))) for i in range(n.bit_length() - 1)]
    far = list(range(n - 1, 0, -1))
    half = n // 4
    near = far[: 2 * half]
    order = [k for pair in zip(near[:half], near[half:]) for k in pair] + far[2 * half :]
    return {k: me + sum(step for bit, step in flips if k & bit) for k in order}


def over_tiles(start, count, body, carry=0):
    batch = math.gcd(count, 8)

    def step(i, held):
        for j in range(batch):
            t = start + i * batch + j
            held = body(t, pl.ds(pl.multiple_of(t * LANES, LANES), LANES), held)
        return held

    return lax.fori_loop(0, count // batch, step, carry)


def wait_bytes(ref, sem):
    pltpu.make_async_copy(ref, ref, sem).wait()


def kernel(
    n, groups, rows, width, parts, z_parts,
    grads, momentum, worker_error, server_error,
    synced, werr_out, serr_out,
    g_in, m_in, e_in, se_in, blend, decoded_in, by_row, entry,
    send, got, zbuf, gathered,
    in_sem, row_sem, z_sem, ag_sem,
):
    me, grp = lax.axis_index("dp"), lax.axis_index("grp")
    tiles = width // LANES
    part, z_part = tiles // parts, tiles // z_parts

    halves = 2
    half = width // halves
    grads_load = pltpu.make_async_copy(grads, g_in, in_sem.at[0])
    server_load = pltpu.make_async_copy(server_error, se_in, in_sem.at[1])
    loads = [
        [
            pltpu.make_async_copy(
                src.at[:, pl.ds(h * half, half)], dst.at[:, pl.ds(h * half, half)], in_sem.at[2 + 2 * h + i]
            )
            for i, (src, dst) in enumerate(((momentum, m_in), (worker_error, e_in)))
        ]
        for h in range(halves)
    ]
    grads_load.start()
    for pair in loads:
        for load in pair:
            load.start()
    server_load.start()

    mates = partners(me, n)
    others = partners(grp, groups)
    barrier = pltpu.get_barrier_semaphore()
    for to in mates.values():
        pl.semaphore_signal(barrier, inc=1, device_id=(grp, to), device_id_type=MESH)
    for to in others.values():
        pl.semaphore_signal(barrier, inc=1, device_id=(to, me), device_id_type=MESH)

    def push(src, dst, sems, device):
        pltpu.make_async_remote_copy(
            src_ref=src,
            dst_ref=dst,
            send_sem=sems.at[0],
            recv_sem=sems.at[1],
            device_id=device,
            device_id_type=MESH,
        ).start()

    def blend_tile(t, cols, total):
        b = 0.9 * m_in[:, cols] + 0.1 * g_in[:, cols].astype(jnp.float32) + e_in[:, cols]
        blend[:, cols] = b
        return total + jnp.abs(b)

    total = jnp.zeros((rows, LANES), jnp.float32)
    grads_load.wait()
    for h, pair in enumerate(loads):
        for load in pair:
            load.wait()
        total = over_tiles(h * (tiles // halves), tiles // halves, blend_tile, total)
    mean = jnp.sum(total, axis=1, keepdims=True) / width
    scale = (mean + 1e-6).astype(jnp.bfloat16).astype(jnp.float32)
    inverse = jnp.broadcast_to(1.0 / scale, (rows, LANES))
    scale = jnp.broadcast_to(scale, (rows, LANES))

    def block_of(p, r):
        return pl.ds(pl.multiple_of((p * rows + r) * part, part), part)

    for p in range(parts):

        def decode_tile(t, cols, held):
            c = jnp.tanh(blend[:, cols] * inverse).astype(jnp.bfloat16).astype(jnp.float32)
            c = scale * c
            decoded_in[:, cols] = c
            by_row[pl.ds(p * (rows - 1) * part + t, rows, stride=part), :] = c
            return held

        over_tiles(p * part, part, decode_tile)
        for k, to in mates.items():
            send[p, k - 1] = by_row[block_of(p, to), :].astype(jnp.bfloat16)

    pl.semaphore_wait(barrier, n - 1 + groups - 1)
    for p in range(parts):
        for k, to in mates.items():
            push(send.at[p, k - 1], got.at[p, k - 1], row_sem.at[p], (grp, to))

    def error_tile(t, cols, held):
        werr_out[:, cols] = blend[:, cols] - decoded_in[:, cols]
        return held

    over_tiles(0, tiles, error_tile)
    server_load.wait()

    size = jnp.zeros((part, LANES), jnp.float32)
    for p in range(parts):
        here = slice(p * part, (p + 1) * part)
        summed = by_row[block_of(p, me), :]
        wait_bytes(got.at[p], row_sem.at[p, 1])
        for k in range(n - 1):
            summed = summed + got[p, k].astype(jnp.float32)
        summed = summed / n + se_in[here, :]
        entry[here, :] = summed
        size = size + jnp.abs(summed)
    mean = jnp.sum(jnp.sum(size, axis=0, keepdims=True), axis=1, keepdims=True) / width
    s_scale = (mean + 1e-6).astype(jnp.bfloat16).astype(jnp.float32)
    s_inverse = 1.0 / s_scale
    for p in range(z_parts):
        here = slice(p * z_part, (p + 1) * z_part)
        s_code = jnp.tanh(entry[here, :] * s_inverse).astype(jnp.bfloat16).astype(jnp.float32)
        decoded = s_scale * s_code
        zbuf[p, grp] = decoded.astype(jnp.bfloat16)
        for to in others.values():
            push(zbuf.at[p, grp], zbuf.at[p, grp], z_sem.at[p], (to, me))
        serr_out[here, :] = entry[here, :] - decoded

    for p in range(z_parts):
        if groups > 1:
            wait_bytes(zbuf.at[p, pl.ds(0, groups - 1)], z_sem.at[p, 1])
        mixed = zbuf[p, 0].astype(jnp.float32)
        for g in range(1, groups):
            mixed = mixed + zbuf[p, g].astype(jnp.float32)
        gathered[p, me] = (mixed / groups).astype(jnp.bfloat16)
        for to in mates.values():
            push(gathered.at[p, me], gathered.at[p, me], ag_sem.at[p], (grp, to))

    for p in range(parts):
        wait_bytes(got.at[p], row_sem.at[p, 0])
    if groups > 1:
        for p in range(z_parts):
            wait_bytes(zbuf.at[p, pl.ds(0, groups - 1)], z_sem.at[p, 0])

    for p in range(z_parts):
        wait_bytes(gathered.at[p, pl.ds(0, n - 1)], ag_sem.at[p, 1])
        base = p * rows * z_part
        for r in range(n):
            by_row[base + r * z_part : base + (r + 1) * z_part, :] = gathered[p, r].astype(jnp.float32)

        def synced_tile(t, cols, held):
            synced[:, cols] = by_row[pl.ds(base - p * z_part + t, rows, stride=z_part), :]
            return held

        over_tiles(p * z_part, z_part, synced_tile)

    for p in range(z_parts):
        wait_bytes(gathered.at[p, pl.ds(0, n - 1)], ag_sem.at[p, 0])


def store(synced, werr, serr, synced_out, werr_out, serr_out, sem):
    copies = [
        pltpu.make_async_copy(src, dst, sem.at[i])
        for i, (src, dst) in enumerate(((synced, synced_out), (werr, werr_out), (serr, serr_out)))
    ]
    for copy in copies:
        copy.start()
    for copy in copies:
        copy.wait()


def solution(mesh):
    n, groups = mesh.shape["dp"], mesh.shape["grp"]

    def per_device(grads, momentum, worker_error, server_error):
        rows, width = grads.shape[2:]
        assert rows == n
        tiles = width // LANES
        parts, z_parts = 1, 2
        part_block = (tiles // parts, LANES)
        z_block = (tiles // z_parts, LANES)
        f32, bf16 = jnp.float32, jnp.bfloat16
        whole = (rows, width)
        block = (tiles, LANES)
        in_hbm = pl.BlockSpec(memory_space=pltpu.HBM)
        in_vmem = pl.BlockSpec(memory_space=pltpu.VMEM)
        anywhere = pl.BlockSpec(memory_space=pl.ANY)
        pinned = functools.partial(pltpu.with_memory_space_constraint, memory_space=pltpu.HBM)
        synced, werr, serr = pl.pallas_call(
            functools.partial(kernel, n, groups, rows, width, parts, z_parts),
            out_shape=(
                jax.ShapeDtypeStruct(whole, f32),
                jax.ShapeDtypeStruct(whole, f32),
                jax.ShapeDtypeStruct(block, f32),
            ),
            in_specs=[anywhere] * 4,
            out_specs=(in_vmem,) * 3,
            scratch_shapes=[
                pltpu.VMEM(whole, bf16),
                pltpu.VMEM(whole, f32),
                pltpu.VMEM(whole, f32),
                pltpu.VMEM(block, f32),
                pltpu.VMEM(whole, f32),
                pltpu.VMEM(whole, f32),
                pltpu.VMEM((rows * tiles, LANES), f32),
                pltpu.VMEM(block, f32),
                pltpu.VMEM((parts, n - 1) + part_block, bf16),
                pltpu.VMEM((parts, n - 1) + part_block, bf16),
                pltpu.VMEM((z_parts, groups) + z_block, bf16),
                pltpu.VMEM((z_parts, n) + z_block, bf16),
                pltpu.SemaphoreType.DMA((6,)),
                pltpu.SemaphoreType.DMA((parts, 2)),
                pltpu.SemaphoreType.DMA((z_parts, 2)),
                pltpu.SemaphoreType.DMA((z_parts, 2)),
            ],
            compiler_params=pltpu.CompilerParams(
                collective_id=0, has_side_effects=True, vmem_limit_bytes=48 * 2**20
            ),
            name="sync",
        )(
            pinned(grads.reshape(whole)),
            pinned(momentum.reshape(whole)),
            pinned(worker_error.reshape(whole)),
            pinned(server_error.reshape(block)),
        )
        synced, werr, serr = pl.pallas_call(
            store,
            out_shape=tuple(jax.ShapeDtypeStruct(x.shape, f32) for x in (synced, werr, serr)),
            in_specs=[anywhere] * 3,
            out_specs=(in_hbm,) * 3,
            scratch_shapes=[pltpu.SemaphoreType.DMA((3,))],
            compiler_params=pltpu.CompilerParams(vmem_limit_bytes=2**20),
            name="store",
        )(synced, werr, serr)
        return synced, werr.reshape(momentum.shape), serr.reshape(server_error.shape)

    placed = (
        P("grp", "dp", None, None),
        P("grp", "dp", None, None),
        P("grp", "dp", None, None),
        P("grp", "dp", None),
    )
    return jax.shard_map(
        per_device,
        mesh=mesh,
        in_specs=placed,
        out_specs=(P(), P("grp", "dp", None, None), P("grp", "dp", None)),
        check_vma=False,
    )
```

```python
import functools
import math

import jax
import jax.numpy as jnp
from jax import lax
from jax.experimental import pallas as pl
from jax.experimental.pallas import tpu as pltpu
from jax.sharding import PartitionSpec as P

MESH = pl.DeviceIdType.MESH
LANES = 128


def partners(me, n):
    if n & (n - 1):
        return {k: lax.rem(me + k, n) for k in range(n - 1, 0, -1)}
    flips = [(1 << i, (1 << i) * (1 - 2 * lax.rem(lax.div(me, 1 << i), 2))) for i in range(n.bit_length() - 1)]
    far = list(range(n - 1, 0, -1))
    half = n // 4
    near = far[: 2 * half]
    order = [k for pair in zip(near[:half], near[half:]) for k in pair] + far[2 * half :]
    return {k: me + sum(step for bit, step in flips if k & bit) for k in order}


def over_tiles(start, count, body, carry=0):
    batch = math.gcd(count, 8)

    def step(i, held):
        for j in range(batch):
            t = start + i * batch + j
            held = body(t, pl.ds(pl.multiple_of(t * LANES, LANES), LANES), held)
        return held

    return lax.fori_loop(0, count // batch, step, carry)


def wait_bytes(ref, sem):
    pltpu.make_async_copy(ref, ref, sem).wait()


def kernel(
    n, groups, rows, width, parts, z_parts,
    grads, momentum, worker_error, server_error,
    synced, werr_out, serr_out,
    g_in, m_in, e_in, se_in, blend, decoded_in, by_row, entry,
    send, got, zbuf, gathered,
    in_sem, row_sem, z_sem, ag_sem,
):
    me, grp = lax.axis_index("dp"), lax.axis_index("grp")
    tiles = width // LANES
    part, z_part = tiles // parts, tiles // z_parts

    halves = 2
    half = width // halves
    grads_load = pltpu.make_async_copy(grads, g_in, in_sem.at[0])
    server_load = pltpu.make_async_copy(server_error, se_in, in_sem.at[1])
    loads = [
        [
            pltpu.make_async_copy(
                src.at[:, pl.ds(h * half, half)], dst.at[:, pl.ds(h * half, half)], in_sem.at[2 + 2 * h + i]
            )
            for i, (src, dst) in enumerate(((momentum, m_in), (worker_error, e_in)))
        ]
        for h in range(halves)
    ]
    grads_load.start()
    for pair in loads:
        for load in pair:
            load.start()
    server_load.start()

    mates = partners(me, n)
    others = partners(grp, groups)
    barrier = pltpu.get_barrier_semaphore()
    for to in mates.values():
        pl.semaphore_signal(barrier, inc=1, device_id=(grp, to), device_id_type=MESH)
    for to in others.values():
        pl.semaphore_signal(barrier, inc=1, device_id=(to, me), device_id_type=MESH)

    def push(src, dst, sems, device):
        pltpu.make_async_remote_copy(
            src_ref=src,
            dst_ref=dst,
            send_sem=sems.at[0],
            recv_sem=sems.at[1],
            device_id=device,
            device_id_type=MESH,
        ).start()

    def blend_tile(t, cols, total):
        b = 0.9 * m_in[:, cols] + 0.1 * g_in[:, cols].astype(jnp.float32) + e_in[:, cols]
        blend[:, cols] = b
        return total + jnp.abs(b)

    total = jnp.zeros((rows, LANES), jnp.float32)
    grads_load.wait()
    for h, pair in enumerate(loads):
        for load in pair:
            load.wait()
        total = over_tiles(h * (tiles // halves), tiles // halves, blend_tile, total)
    mean = jnp.sum(total, axis=1, keepdims=True) / width
    scale = (mean + 1e-6).astype(jnp.bfloat16).astype(jnp.float32)
    inverse = jnp.broadcast_to(1.0 / scale, (rows, LANES))
    scale = jnp.broadcast_to(scale, (rows, LANES))

    def block_of(p, r):
        return pl.ds(pl.multiple_of((p * rows + r) * part, part), part)

    for p in range(parts):

        def decode_tile(t, cols, held):
            c = jnp.tanh(blend[:, cols] * inverse).astype(jnp.bfloat16).astype(jnp.float32)
            c = scale * c
            decoded_in[:, cols] = c
            by_row[pl.ds(p * (rows - 1) * part + t, rows, stride=part), :] = c
            return held

        over_tiles(p * part, part, decode_tile)
        for k, to in mates.items():
            send[p, k - 1] = by_row[block_of(p, to), :].astype(jnp.bfloat16)

    pl.semaphore_wait(barrier, n - 1 + groups - 1)
    for p in range(parts):
        for k, to in mates.items():
            push(send.at[p, k - 1], got.at[p, k - 1], row_sem.at[p], (grp, to))

    def error_tile(t, cols, held):
        werr_out[:, cols] = blend[:, cols] - decoded_in[:, cols]
        return held

    over_tiles(0, tiles, error_tile)
    server_load.wait()

    size = jnp.zeros((part, LANES), jnp.float32)
    for p in range(parts):
        here = slice(p * part, (p + 1) * part)
        summed = by_row[block_of(p, me), :]
        wait_bytes(got.at[p], row_sem.at[p, 1])
        for k in range(n - 1):
            summed = summed + got[p, k].astype(jnp.float32)
        summed = summed / n + se_in[here, :]
        entry[here, :] = summed
        size = size + jnp.abs(summed)
    mean = jnp.sum(jnp.sum(size, axis=0, keepdims=True), axis=1, keepdims=True) / width
    s_scale = (mean + 1e-6).astype(jnp.bfloat16).astype(jnp.float32)
    s_inverse = 1.0 / s_scale
    for p in range(z_parts):
        here = slice(p * z_part, (p + 1) * z_part)
        s_code = jnp.tanh(entry[here, :] * s_inverse).astype(jnp.bfloat16).astype(jnp.float32)
        decoded = s_scale * s_code
        zbuf[p, grp] = decoded.astype(jnp.bfloat16)
        for to in others.values():
            push(zbuf.at[p, grp], zbuf.at[p, grp], z_sem.at[p], (to, me))
        serr_out[here, :] = entry[here, :] - decoded

    for p in range(z_parts):
        if groups > 1:
            wait_bytes(zbuf.at[p, pl.ds(0, groups - 1)], z_sem.at[p, 1])
        mixed = zbuf[p, 0].astype(jnp.float32)
        for g in range(1, groups):
            mixed = mixed + zbuf[p, g].astype(jnp.float32)
        gathered[p, me] = (mixed / groups).astype(jnp.bfloat16)
        for to in mates.values():
            push(gathered.at[p, me], gathered.at[p, me], ag_sem.at[p], (grp, to))

    for p in range(parts):
        wait_bytes(got.at[p], row_sem.at[p, 0])
    if groups > 1:
        for p in range(z_parts):
            wait_bytes(zbuf.at[p, pl.ds(0, groups - 1)], z_sem.at[p, 0])

    for p in range(z_parts):
        wait_bytes(gathered.at[p, pl.ds(0, n - 1)], ag_sem.at[p, 1])
        base = p * rows * z_part
        for r in range(n):
            by_row[base + r * z_part : base + (r + 1) * z_part, :] = gathered[p, r].astype(jnp.float32)

        def synced_tile(t, cols, held):
            synced[:, cols] = by_row[pl.ds(base - p * z_part + t, rows, stride=z_part), :]
            return held

        over_tiles(p * z_part, z_part, synced_tile)

    for p in range(z_parts):
        wait_bytes(gathered.at[p, pl.ds(0, n - 1)], ag_sem.at[p, 0])


def store(synced, werr, serr, synced_out, werr_out, serr_out, sem):
    copies = [
        pltpu.make_async_copy(src, dst, sem.at[i])
        for i, (src, dst) in enumerate(((synced, synced_out), (werr, werr_out), (serr, serr_out)))
    ]
    for copy in copies:
        copy.start()
    for copy in copies:
        copy.wait()


def solution(mesh):
    n, groups = mesh.shape["dp"], mesh.shape["grp"]

    def per_device(grads, momentum, worker_error, server_error):
        rows, width = grads.shape[2:]
        assert rows == n
        tiles = width // LANES
        parts, z_parts = 1, 1
        part_block = (tiles // parts, LANES)
        z_block = (tiles // z_parts, LANES)
        f32, bf16 = jnp.float32, jnp.bfloat16
        whole = (rows, width)
        block = (tiles, LANES)
        in_hbm = pl.BlockSpec(memory_space=pltpu.HBM)
        in_vmem = pl.BlockSpec(memory_space=pltpu.VMEM)
        anywhere = pl.BlockSpec(memory_space=pl.ANY)
        pinned = functools.partial(pltpu.with_memory_space_constraint, memory_space=pltpu.HBM)
        synced, werr, serr = pl.pallas_call(
            functools.partial(kernel, n, groups, rows, width, parts, z_parts),
            out_shape=(
                jax.ShapeDtypeStruct(whole, f32),
                jax.ShapeDtypeStruct(whole, f32),
                jax.ShapeDtypeStruct(block, f32),
            ),
            in_specs=[anywhere] * 4,
            out_specs=(in_vmem,) * 3,
            scratch_shapes=[
                pltpu.VMEM(whole, bf16),
                pltpu.VMEM(whole, f32),
                pltpu.VMEM(whole, f32),
                pltpu.VMEM(block, f32),
                pltpu.VMEM(whole, f32),
                pltpu.VMEM(whole, f32),
                pltpu.VMEM((rows * tiles, LANES), f32),
                pltpu.VMEM(block, f32),
                pltpu.VMEM((parts, n - 1) + part_block, bf16),
                pltpu.VMEM((parts, n - 1) + part_block, bf16),
                pltpu.VMEM((z_parts, groups) + z_block, bf16),
                pltpu.VMEM((z_parts, n) + z_block, bf16),
                pltpu.SemaphoreType.DMA((6,)),
                pltpu.SemaphoreType.DMA((parts, 2)),
                pltpu.SemaphoreType.DMA((z_parts, 2)),
                pltpu.SemaphoreType.DMA((z_parts, 2)),
            ],
            compiler_params=pltpu.CompilerParams(
                collective_id=0, has_side_effects=True, vmem_limit_bytes=48 * 2**20
            ),
            name="sync",
        )(
            pinned(grads.reshape(whole)),
            pinned(momentum.reshape(whole)),
            pinned(worker_error.reshape(whole)),
            pinned(server_error.reshape(block)),
        )
        synced, werr, serr = pl.pallas_call(
            store,
            out_shape=tuple(jax.ShapeDtypeStruct(x.shape, f32) for x in (synced, werr, serr)),
            in_specs=[anywhere] * 3,
            out_specs=(in_hbm,) * 3,
            scratch_shapes=[pltpu.SemaphoreType.DMA((3,))],
            compiler_params=pltpu.CompilerParams(vmem_limit_bytes=2**20),
            name="store",
        )(synced, werr, serr)
        return synced, werr.reshape(momentum.shape), serr.reshape(server_error.shape)

    placed = (
        P("grp", "dp", None, None),
        P("grp", "dp", None, None),
        P("grp", "dp", None, None),
        P("grp", "dp", None),
    )
    return jax.shard_map(
        per_device,
        mesh=mesh,
        in_specs=placed,
        out_specs=(P(), P("grp", "dp", None, None), P("grp", "dp", None)),
        check_vma=False,
    )
```

```python
import functools
import math

import jax
import jax.numpy as jnp
from jax import lax
from jax.experimental import pallas as pl
from jax.experimental.pallas import tpu as pltpu
from jax.sharding import PartitionSpec as P

MESH = pl.DeviceIdType.MESH
LANES = 128


def partners(me, n):
    if n & (n - 1):
        return {k: lax.rem(me + k, n) for k in range(n - 1, 0, -1)}
    flips = [(1 << i, (1 << i) * (1 - 2 * lax.rem(lax.div(me, 1 << i), 2))) for i in range(n.bit_length() - 1)]
    far = list(range(n - 1, 0, -1))
    half = n // 4
    near = far[: 2 * half]
    order = [k for pair in zip(near[:half], near[half:]) for k in pair] + far[2 * half :]
    return {k: me + sum(step for bit, step in flips if k & bit) for k in order}


def over_tiles(start, count, body, carry=0):
    batch = math.gcd(count, 8)

    def step(i, held):
        for j in range(batch):
            t = start + i * batch + j
            held = body(t, pl.ds(pl.multiple_of(t * LANES, LANES), LANES), held)
        return held

    return lax.fori_loop(0, count // batch, step, carry)


def wait_bytes(ref, sem):
    pltpu.make_async_copy(ref, ref, sem).wait()


def kernel(
    n, groups, rows, width, parts, z_parts,
    grads, momentum, worker_error, server_error,
    synced, werr_out, serr_out,
    g_in, m_in, e_in, se_in, blend, decoded_in, by_row, entry,
    send, got, zbuf, gathered,
    in_sem, row_sem, z_sem, ag_sem,
):
    me, grp = lax.axis_index("dp"), lax.axis_index("grp")
    tiles = width // LANES
    part, z_part = tiles // parts, tiles // z_parts

    halves = 2
    half = width // halves
    grads_load = pltpu.make_async_copy(grads, g_in, in_sem.at[0])
    server_load = pltpu.make_async_copy(server_error, se_in, in_sem.at[1])
    loads = [
        [
            pltpu.make_async_copy(
                src.at[:, pl.ds(h * half, half)], dst.at[:, pl.ds(h * half, half)], in_sem.at[2 + 2 * h + i]
            )
            for i, (src, dst) in enumerate(((momentum, m_in), (worker_error, e_in)))
        ]
        for h in range(halves)
    ]
    mates = partners(me, n)
    others = partners(grp, groups)
    barrier = pltpu.get_barrier_semaphore()
    for to in mates.values():
        pl.semaphore_signal(barrier, inc=1, device_id=(grp, to), device_id_type=MESH)
    for to in others.values():
        pl.semaphore_signal(barrier, inc=1, device_id=(to, me), device_id_type=MESH)
    grads_load.start()
    for pair in loads:
        for load in pair:
            load.start()
    server_load.start()

    def push(src, dst, sems, device):
        pltpu.make_async_remote_copy(
            src_ref=src,
            dst_ref=dst,
            send_sem=sems.at[0],
            recv_sem=sems.at[1],
            device_id=device,
            device_id_type=MESH,
        ).start()

    def blend_tile(t, cols, total):
        b = 0.9 * m_in[:, cols] + 0.1 * g_in[:, cols].astype(jnp.float32) + e_in[:, cols]
        blend[:, cols] = b
        return total + jnp.abs(b)

    total = jnp.zeros((rows, LANES), jnp.float32)
    grads_load.wait()
    for h, pair in enumerate(loads):
        for load in pair:
            load.wait()
        total = over_tiles(h * (tiles // halves), tiles // halves, blend_tile, total)
    mean = jnp.sum(total, axis=1, keepdims=True) / width
    scale = (mean + 1e-6).astype(jnp.bfloat16).astype(jnp.float32)
    inverse = jnp.broadcast_to(1.0 / scale, (rows, LANES))
    scale = jnp.broadcast_to(scale, (rows, LANES))

    def block_of(p, r):
        return pl.ds(pl.multiple_of((p * rows + r) * part, part), part)

    for p in range(parts):

        def decode_tile(t, cols, held):
            c = jnp.tanh(blend[:, cols] * inverse).astype(jnp.bfloat16).astype(jnp.float32)
            c = scale * c
            decoded_in[:, cols] = c
            by_row[pl.ds(p * (rows - 1) * part + t, rows, stride=part), :] = c
            return held

        over_tiles(p * part, part, decode_tile)
        for k, to in mates.items():
            send[p, k - 1] = by_row[block_of(p, to), :].astype(jnp.bfloat16)

    pl.semaphore_wait(barrier, n - 1 + groups - 1)
    for p in range(parts):
        for k, to in mates.items():
            push(send.at[p, k - 1], got.at[p, k - 1], row_sem.at[p], (grp, to))

    def error_tile(t, cols, held):
        werr_out[:, cols] = blend[:, cols] - decoded_in[:, cols]
        return held

    over_tiles(0, tiles, error_tile)
    server_load.wait()

    size = jnp.zeros((part, LANES), jnp.float32)
    for p in range(parts):
        here = slice(p * part, (p + 1) * part)
        summed = by_row[block_of(p, me), :]
        wait_bytes(got.at[p], row_sem.at[p, 1])
        for k in range(n - 1):
            summed = summed + got[p, k].astype(jnp.float32)
        summed = summed / n + se_in[here, :]
        entry[here, :] = summed
        size = size + jnp.abs(summed)
    mean = jnp.sum(jnp.sum(size, axis=0, keepdims=True), axis=1, keepdims=True) / width
    s_scale = (mean + 1e-6).astype(jnp.bfloat16).astype(jnp.float32)
    s_inverse = 1.0 / s_scale
    for p in range(z_parts):
        here = slice(p * z_part, (p + 1) * z_part)
        s_code = jnp.tanh(entry[here, :] * s_inverse).astype(jnp.bfloat16).astype(jnp.float32)
        decoded = s_scale * s_code
        zbuf[p, grp] = decoded.astype(jnp.bfloat16)
        for to in others.values():
            push(zbuf.at[p, grp], zbuf.at[p, grp], z_sem.at[p], (to, me))
        serr_out[here, :] = entry[here, :] - decoded

    for p in range(z_parts):
        if groups > 1:
            wait_bytes(zbuf.at[p, pl.ds(0, groups - 1)], z_sem.at[p, 1])
        mixed = zbuf[p, 0].astype(jnp.float32)
        for g in range(1, groups):
            mixed = mixed + zbuf[p, g].astype(jnp.float32)
        gathered[p, me] = (mixed / groups).astype(jnp.bfloat16)
        for to in mates.values():
            push(gathered.at[p, me], gathered.at[p, me], ag_sem.at[p], (grp, to))

    for p in range(parts):
        wait_bytes(got.at[p], row_sem.at[p, 0])
    if groups > 1:
        for p in range(z_parts):
            wait_bytes(zbuf.at[p, pl.ds(0, groups - 1)], z_sem.at[p, 0])

    for p in range(z_parts):
        wait_bytes(gathered.at[p, pl.ds(0, n - 1)], ag_sem.at[p, 1])
        base = p * rows * z_part
        for r in range(n):
            by_row[base + r * z_part : base + (r + 1) * z_part, :] = gathered[p, r].astype(jnp.float32)

        def synced_tile(t, cols, held):
            synced[:, cols] = by_row[pl.ds(base - p * z_part + t, rows, stride=z_part), :]
            return held

        over_tiles(p * z_part, z_part, synced_tile)

    for p in range(z_parts):
        wait_bytes(gathered.at[p, pl.ds(0, n - 1)], ag_sem.at[p, 0])


def store(synced, werr, serr, synced_out, werr_out, serr_out, sem):
    copies = [
        pltpu.make_async_copy(src, dst, sem.at[i])
        for i, (src, dst) in enumerate(((synced, synced_out), (werr, werr_out), (serr, serr_out)))
    ]
    for copy in copies:
        copy.start()
    for copy in copies:
        copy.wait()


def solution(mesh):
    n, groups = mesh.shape["dp"], mesh.shape["grp"]

    def per_device(grads, momentum, worker_error, server_error):
        rows, width = grads.shape[2:]
        assert rows == n
        tiles = width // LANES
        parts, z_parts = 1, 1
        part_block = (tiles // parts, LANES)
        z_block = (tiles // z_parts, LANES)
        f32, bf16 = jnp.float32, jnp.bfloat16
        whole = (rows, width)
        block = (tiles, LANES)
        in_hbm = pl.BlockSpec(memory_space=pltpu.HBM)
        in_vmem = pl.BlockSpec(memory_space=pltpu.VMEM)
        anywhere = pl.BlockSpec(memory_space=pl.ANY)
        pinned = functools.partial(pltpu.with_memory_space_constraint, memory_space=pltpu.HBM)
        synced, werr, serr = pl.pallas_call(
            functools.partial(kernel, n, groups, rows, width, parts, z_parts),
            out_shape=(
                jax.ShapeDtypeStruct(whole, f32),
                jax.ShapeDtypeStruct(whole, f32),
                jax.ShapeDtypeStruct(block, f32),
            ),
            in_specs=[anywhere] * 4,
            out_specs=(in_vmem,) * 3,
            scratch_shapes=[
                pltpu.VMEM(whole, bf16),
                pltpu.VMEM(whole, f32),
                pltpu.VMEM(whole, f32),
                pltpu.VMEM(block, f32),
                pltpu.VMEM(whole, f32),
                pltpu.VMEM(whole, f32),
                pltpu.VMEM(((rows + 1) * tiles, LANES), f32),
                pltpu.VMEM(block, f32),
                pltpu.VMEM((parts, n - 1) + part_block, bf16),
                pltpu.VMEM((parts, n - 1) + part_block, bf16),
                pltpu.VMEM((z_parts, groups) + z_block, bf16),
                pltpu.VMEM((z_parts, n) + z_block, bf16),
                pltpu.SemaphoreType.DMA((6,)),
                pltpu.SemaphoreType.DMA((parts, 2)),
                pltpu.SemaphoreType.DMA((z_parts, 2)),
                pltpu.SemaphoreType.DMA((z_parts, 2)),
            ],
            compiler_params=pltpu.CompilerParams(
                collective_id=0, has_side_effects=True, vmem_limit_bytes=48 * 2**20
            ),
            name="sync",
        )(
            pinned(grads.reshape(whole)),
            pinned(momentum.reshape(whole)),
            pinned(worker_error.reshape(whole)),
            pinned(server_error.reshape(block)),
        )
        synced, werr, serr = pl.pallas_call(
            store,
            out_shape=tuple(jax.ShapeDtypeStruct(x.shape, f32) for x in (synced, werr, serr)),
            in_specs=[anywhere] * 3,
            out_specs=(in_hbm,) * 3,
            scratch_shapes=[pltpu.SemaphoreType.DMA((3,))],
            compiler_params=pltpu.CompilerParams(vmem_limit_bytes=2**20),
            name="store",
        )(synced, werr, serr)
        return synced, werr.reshape(momentum.shape), serr.reshape(server_error.shape)

    placed = (
        P("grp", "dp", None, None),
        P("grp", "dp", None, None),
        P("grp", "dp", None, None),
        P("grp", "dp", None),
    )
    return jax.shard_map(
        per_device,
        mesh=mesh,
        in_specs=placed,
        out_specs=(P(), P("grp", "dp", None, None), P("grp", "dp", None)),
        check_vma=False,
    )
```
